256 devices in a mesh: row: 16 (over z, core), col: 16 (over x, y).
Axes of the slice: x: 4, y: 4, z: 8, core: 2. Of those that a mesh axis runs over, the one named last changes fastest.
Arguments:
- student: bfloat16 [14336, 1024], P(('row', 'col')), may hold values from -0.5 to 0.5
- teacher: bfloat16 [14336, 4096], P(('row', 'col')), may hold values from -0.125 to 0.125
- scales: float32 [14336], P(('row', 'col')), may hold values from 0.3 to 3
Outputs:
- student_grad: float32 [14336, 1024], P(('row', 'col'))
The draws below stay inside these ranges and needn't reach their ends.
All inputs are finite; a program needn't handle non-finite values.
Results may differ from the reference program's by a relative error of at most 0.004.
Values may be sent and summed in bfloat16 or wider, within the bound.
A program may use at most 64 MiB of HBM per device.

```python
import math
import jax
import jax.numpy as jnp
from jax import lax

DS = 1024
DT = 4096
ROWS_DEV = 56
TEXTS = 14336
N_ROW = 16
N_COL = 16


def block_levels(own_key, dims, pieces, low, high):
    def one(position, shards_of):
        steps = jax.random.uniform(jax.random.fold_in(jax.random.fold_in(own_key, 6), position), (shards_of,), jnp.float32, low / len(pieces), high / len(pieces))
        return jnp.repeat(jnp.exp(steps), dims[position] // shards_of).reshape((-1,) + (1,) * (len(dims) - position - 1))

    gain = one(*pieces[0])
    for cut in pieces[1:]:
        gain = gain * one(*cut)
    return gain


def centred(key, extent, scale, most, shards=(), kind=jnp.bfloat16):
    factor_of = block_levels(key, extent, shards, -0.22, 0.18) if shards else 1.0
    drawn = jax.random.normal(key, extent, jnp.float32) * scale * factor_of
    return jnp.minimum(jnp.maximum(drawn, -most), most).astype(kind)


def setup_inputs(seed: int = 0) -> dict:
    key_list = jax.random.split(jax.random.key(seed), 4)
    return {
        "student": centred(key_list[0], (TEXTS, DS), 0.0625, 0.5, ((0, 256),)),
        "teacher": centred(key_list[1], (TEXTS, DT), 0.015625, 0.125, ((0, 256),)),
        "scales": jnp.clip(jnp.exp(math.log(3.0) - 2.3025851 * jax.random.uniform(key_list[2], (TEXTS,), jnp.float32) ** block_levels(key_list[2], (TEXTS,), ((0, 256),), -0.2, 0.2)), 0.3, 3.0),
    }


def reference(student, teacher, scales):
    block_rows = ROWS_DEV * N_COL
    factor = 4.0 / jnp.sqrt(jnp.float32(TEXTS))

    def one_block(index):
        start = (index * block_rows).astype(jnp.int32)
        part_student = lax.dynamic_slice_in_dim(student, start, block_rows, 0)
        part_teacher = lax.dynamic_slice_in_dim(teacher, start, block_rows, 0)
        part_scales = lax.dynamic_slice_in_dim(scales, start, block_rows, 0)
        student_gram = jnp.dot(part_student, student.T, preferred_element_type=jnp.float32)
        teacher_dots = jnp.dot(part_teacher, teacher.T, preferred_element_type=jnp.float32)
        teacher_gram = teacher_dots * part_scales[:, None] * scales[None, :]
        difference = jnp.clip(student_gram - teacher_gram, -0.25, 0.25).astype(jnp.bfloat16)
        return factor * jnp.dot(difference, student, preferred_element_type=jnp.float32)
    blocks = lax.map(one_block, jnp.arange(N_ROW, dtype=jnp.int32))
    return blocks.reshape(TEXTS, DS)
```

```python
import functools
import jax
import jax.numpy as jnp
from jax import lax
from jax.experimental import pallas as pl
from jax.experimental.pallas import tpu as pltpu
from jax.sharding import PartitionSpec as P

DS, DT, ROWS, EXT = 1024, 4096, 56, 128
TEXTS = 14336
WIDTH = DT + DS + EXT
PIECES = ((0, 1280), (1280, 2560), (2560, 3840), (3840, WIDTH))
T_PIECES = ((0, 1280), (1280, 2560), (2560, 3840), (3840, DT))
LINKS = ("X+", "X-", "Y+", "Y-", "Z+", "Z-", "S")
GROUP = 4 * ROWS
WI = 512
WJ = DS - WI
QI, HJ = WI // 4, WJ // 2
LAG = 3
BUDGET = 1.5
RLAG = 4


def moved(block, link):
    step = 1 if link[1] == "+" else -1
    if link[0] == "X":
        return ((block[0] - step) % 4, block[1])
    return (block[0], (block[1] - step) % 4)


def gather_xy():
    out = []

    def ring(axis, heads, p, q):
        for head in heads:
            for link, far, order in ((axis + "+", p, (p, q)), (axis + "-", q, (q, p))):
                near = moved(head, link)
                out.extend((link, head, piece, near) for piece in order)
                out.append((link, near, far, moved(near, link)))

    ring("X", [(0, 0)], 0, 1)
    ring("Y", [(d, 0) for d in (0, 1, 3, 2)], 0, 1)
    ring("Y", [(0, 0)], 2, 3)
    ring("X", [(0, d) for d in (0, 1, 3, 2)], 2, 3)
    return out


def slots_of(moves, feeds, links, lag):
    n = len(moves)
    users = [[j for j in range(n) if i in feeds[j]] for i in range(n)]

    @functools.cache
    def height(i):
        return 1 + max([height(j) for j in users[i]], default=0)

    slot, now = {}, 0
    while len(slot) < n:
        now += 1
        for link in links:
            ready = [
                i for i in range(n)
                if i not in slot and moves[i][0] == link
                and all(f in slot and slot[f] + lag <= now for f in feeds[i])
            ]
            if ready:
                best = min(ready, key=lambda i: (-height(i), -len(users[i]), i))
                slot[best] = now
    return slot


def plan_gather():
    moves = gather_xy()
    source = {(m[3], m[2]): i for i, m in enumerate(moves)}
    feeds = [[source[(m[1], m[2])]] if (m[1], m[2]) in source else [] for m in moves]
    slot = slots_of(moves, feeds, LINKS[:4], LAG)
    return moves, feeds, slot


MOVES, FEEDS, SLOT = plan_gather()
LAST = max(SLOT.values())
ARRIVE = {}
for _i, _m in enumerate(MOVES):
    ARRIVE.setdefault(_m[3], {})[_m[2]] = SLOT[_i]
ARRIVE[(0, 0)] = {p: 0 for p in range(4)}
I_ORDER = sorted((b for b in ARRIVE if b != (0, 0)), key=lambda b: (max(ARRIVE[b].values()), sum(ARRIVE[b].values()), b))
I_ORDER = I_ORDER + [(0, 0)]
I_INDEX = {b: i for i, b in enumerate(I_ORDER)}
J_ORDER = [(0, 0), (0, 1), (4, 0), (4, 1)]
for _d in (1, 2, 3):
    J_ORDER += [(_d, 0), (8 - _d, 0), (_d, 1), (8 - _d, 1)]
J_INDEX = {b: 15 + i for i, b in enumerate(J_ORDER)}
BLOCKS = 31

Z_MOVES = []
for _s in range(14):
    _d, _p = _s // 4, _s % 4
    Z_MOVES.append(("Z+", (8 - _d) % 8, _p, 7 - _d, _s + 1))
    Z_MOVES.append(("Z-", _d, (_p + 2) % 4, _d + 1, _s + 1))
J_ARRIVE = {b: {p: 0 for p in range(4)} for b in J_ORDER}
for _m in Z_MOVES:
    J_ARRIVE[(_m[3], 0)][_m[2]] = _m[4]
    J_ARRIVE[(_m[3], 1)][_m[2]] = _m[4] + 1


def plan_compute():
    i_at = [[max(ARRIVE[b][p] for b in I_ORDER[4 * g:4 * g + 4]) for p in range(4)] for g in range(4)]
    j_at = [[max(J_ARRIVE[b][p] for b in J_ORDER[4 * g:4 * g + 4]) for p in range(4)] for g in range(4)]
    left = {(i, j): [0, 1, 2, 3] for i in range(4) for j in range(4)}
    started = set()
    done = {i: 0 for i in range(4)}
    out = {}

    def runs(pieces):
        ranges = []
        for p in pieces:
            if ranges and ranges[-1][1] == T_PIECES[p][0]:
                ranges[-1][1] = T_PIECES[p][1]
            else:
                ranges.append(list(T_PIECES[p]))
        return ranges

    def finish(now, i, j):
        tasks = [("final", i, j, runs(left.pop((i, j))), (i, j) in started)]
        done[i] += 1
        if done[i] == 4:
            tasks.append(("grad", i))
        return tasks

    for now in range(1, LAST + 1):
        seen = now - LAG
        cost, tasks = 0.0, []
        for want in (4, 2, 1):
            for i, j in list(left):
                ready = [p for p in left[(i, j)] if max(i_at[i][p], j_at[j][p]) <= seen]
                if len(ready) == len(left[(i, j)]):
                    if want == 4 and cost < BUDGET:
                        cost += 0.15 + 0.14 * len(ready)
                        tasks += finish(now, i, j)
                    continue
                ready = [p for p in ready if p != 3]
                if want != 4 and len(ready) >= want and cost < BUDGET:
                    tasks.append(("acc", i, j, runs(ready), (i, j) in started))
                    started.add((i, j))
                    left[(i, j)] = [p for p in left[(i, j)] if p not in ready]
                    cost += 0.14 * len(ready)
        out[now] = tasks
    for stage in range(LAST - LAG + 1, LAST + 1):
        tasks = []
        for i, j in sorted(left):
            if max(max(i_at[i]), max(j_at[j])) <= stage:
                tasks += finish(stage, i, j)
        out["after", stage] = tasks
    assert not left
    return out


TASKS = plan_compute()


def plan_reduce():
    moves = []

    def ring(axis, heads, p, q):
        def at(head, d):
            return ((head[0] + d) % 4, head[1]) if axis == "X" else (head[0], (head[1] + d) % 4)
        for head in heads:
            plus, minus = axis + "+", axis + "-"
            moves.append((plus, at(head, 2), p, at(head, 1)))
            moves.append((minus, at(head, 2), q, at(head, 3)))
            for piece in (q, p):
                moves.append((plus, at(head, 1), piece, head))
            for piece in (p, q):
                moves.append((minus, at(head, 3), piece, head))

    ring("Y", [(d, 0) for d in (2, 1, 3, 0)], 0, 1)
    ring("X", [(0, 0)], 0, 1)
    ring("X", [(0, d) for d in (2, 1, 3, 0)], 2, 3)
    ring("Y", [(0, 0)], 2, 3)
    feeds = [[j for j, f in enumerate(moves) if f[3] == m[1] and f[2] == m[2]] for m in moves]
    slot = slots_of(moves, feeds, LINKS[:4], RLAG)
    return moves, feeds, slot


R_MOVES, R_FEEDS, R_SLOT = plan_reduce()
RZ_MOVES = []
for _d in (4, 3, 2, 1):
    RZ_MOVES.append(("Z+", _d, 0, _d - 1))
    RZ_MOVES.append(("Z-", (8 - _d) % 8, 1, (9 - _d) % 8))
    if _d < 4:
        RZ_MOVES.append(("Z+", _d, 1, _d - 1))
        RZ_MOVES.append(("Z-", (8 - _d) % 8, 0, (9 - _d) % 8))
RZ_FEEDS = [[j for j, f in enumerate(RZ_MOVES) if f[3] == m[1] and f[2] == m[2]] for m in RZ_MOVES]


def dot(a, b, dims):
    return lax.dot_general(a, b, ((dims[0], dims[1]), ((), ())), preferred_element_type=jnp.float32)


def kernel(student, teacher, scales, out, X, acc, D, GI, GJ, RI, RJ, RS, load_sem, send, recv):
    row, col = lax.axis_index("row"), lax.axis_index("col")
    z, c = row // 2, row % 2
    x, y = col // 4, col % 4
    peer = {
        "X+": (row, ((x + 1) % 4) * 4 + y), "X-": (row, ((x + 3) % 4) * 4 + y),
        "Y+": (row, x * 4 + (y + 1) % 4), "Y-": (row, x * 4 + (y + 3) % 4),
        "Z+": (((z + 1) % 8) * 2 + c, col), "Z-": (((z + 7) % 8) * 2 + c, col),
        "S": (z * 2 + 1 - c, col),
    }
    loads = [
        pltpu.make_async_copy(teacher, X.at[15, :, pl.ds(0, DT)], load_sem.at[0]),
        pltpu.make_async_copy(student, X.at[15, :, pl.ds(DT, DS)], load_sem.at[1]),
    ]
    for load in loads:
        load.start()
    barrier = pltpu.get_barrier_semaphore()
    for link in LINKS:
        pl.semaphore_signal(barrier, inc=1, device_id=peer[link], device_id_type=pl.DeviceIdType.MESH)
    here = lax.broadcasted_iota(jnp.int32, (ROWS, ROWS), 0) == lax.broadcasted_iota(jnp.int32, (ROWS, ROWS), 1)
    scale = jnp.sum(jnp.where(here, jnp.broadcast_to(scales[...], (ROWS, ROWS)), 0.0), axis=1, keepdims=True)
    high = scale.astype(jnp.bfloat16).astype(jnp.float32)
    mid = (scale - high).astype(jnp.bfloat16).astype(jnp.float32)
    low = scale - high - mid
    lane = lax.broadcasted_iota(jnp.int32, (ROWS, EXT), 1)
    terms = jnp.where(lane == 0, high, jnp.where(lane == 1, mid, jnp.where(lane == 2, low, 0.0)))
    X[15, :, DT + DS:] = terms.astype(jnp.bfloat16)
    for load in loads:
        load.wait()
    pl.semaphore_wait(barrier, len(LINKS))

    copies = []

    def push(link, src, dst):
        n = len(copies)
        copy = pltpu.make_async_remote_copy(
            src_ref=src, dst_ref=dst, send_sem=send.at[n], recv_sem=recv.at[n],
            device_id=peer[link], device_id_type=pl.DeviceIdType.MESH,
        )
        copy.start()
        copies.append(copy)
        return copy

    def part(index, piece):
        low_col, high_col = PIECES[piece]
        return X.at[index, :, pl.ds(low_col, high_col - low_col)]

    def i_rows(g, a, b):
        return X[4 * g:4 * g + 4, :, a:b].reshape(GROUP, b - a)

    def j_rows(g, a, b):
        return X[15 + 4 * g:19 + 4 * g, :, a:b].reshape(GROUP, b - a)

    grads = set()

    def run(task):
        kind, i = task[:2]
        if kind == "grad":
            total = None
            for j in range(4):
                term = dot(D[i, j, :, :GROUP], j_rows(j, DT, DT + WI), ((1,), (0,)))
                total = term if total is None else total + term
            GI[4 * i:4 * i + 4] = total.reshape(4, ROWS, WI)
            for j in range(4):
                term = dot(D[i, j, :, :GROUP], i_rows(i, DT + WI, DT + DS), ((0,), (0,))).reshape(4, ROWS, WJ)
                if grads:
                    GJ[4 * j:4 * j + 4] += term
                else:
                    GJ[4 * j:4 * j + 4] = term
            grads.add(i)
            return
        j, ranges, started = task[2:]
        total = acc[i, j, :, :GROUP] if started else None
        for a, b in ranges:
            term = dot(i_rows(i, a, b), j_rows(j, a, b), ((1,), (1,)))
            total = term if total is None else total + term
        if kind == "acc":
            acc[i, j, :, :GROUP] = total
            return
        own = jnp.sum(i_rows(i, DT + DS, WIDTH).astype(jnp.float32), axis=1, keepdims=True)
        ones = jnp.ones((8, EXT), jnp.bfloat16)
        other = dot(ones, j_rows(j, DT + DS, WIDTH), ((1,), (1,)))[0:1]
        student_gram = dot(i_rows(i, DT, DT + DS), j_rows(j, DT, DT + DS), ((1,), (1,)))
        d = jnp.clip(student_gram - total * own * other, -0.25, 0.25)
        D[i, j, :, :GROUP] = d.astype(jnp.bfloat16)

    arriving, forwards = {}, {}
    first = push("S", X.at[15], X.at[J_INDEX[(0, 1)]])

    def wait_slot(s):
        if s == 0:
            first.wait_recv()
        for copy in forwards.pop(s - 1, []):
            copy.wait_recv()
        for copy in arriving.pop(("xy", s), []):
            copy.wait_recv()
        for copy, m in arriving.pop(("z", s), []):
            copy.wait_recv()
            forwards.setdefault(s, []).append(
                push("S", part(J_INDEX[(m[3], 0)], m[2]), part(J_INDEX[(m[3], 1)], m[2]))
            )

    for now in range(1, LAST + 1):
        if now > LAG - 1:
            wait_slot(now - LAG)
        for i, m in enumerate(MOVES):
            if SLOT[i] == now:
                copy = push(m[0], part(I_INDEX[m[1]], m[2]), part(I_INDEX[m[3]], m[2]))
                arriving.setdefault(("xy", now), []).append(copy)
        for m in Z_MOVES:
            if m[4] == now:
                copy = push(m[0], part(J_INDEX[(m[1], 0)], m[2]), part(J_INDEX[(m[3], 0)], m[2]))
                arriving.setdefault(("z", now), []).append((copy, m))
        for task in TASKS[now]:
            run(task)
    for stage in range(LAST - LAG + 1, LAST + 1):
        wait_slot(stage)
        for task in TASKS["after", stage]:
            run(task)
    assert not arriving and not forwards

    def cols(quarter):
        return pl.ds(quarter * QI, QI)

    def half(h):
        return pl.ds(h * HJ, HJ)

    shared = {}
    for d in (4, 3, 5, 2, 6, 1, 7, 0):
        shared[d] = push("S", GJ.at[J_INDEX[(d, 1)] - 15], RS.at[d])
    waiting = {}

    def collect(i):
        copy = waiting.pop(i)
        copy.wait_recv()
        m = R_MOVES[i]
        GI[I_INDEX[m[3]], :, cols(m[2])] += RI[i]

    def send_xy(i):
        m = R_MOVES[i]
        for f in R_FEEDS[i]:
            if f in waiting:
                collect(f)
        waiting[i] = push(m[0], GI.at[I_INDEX[m[1]], :, cols(m[2])], RI.at[i])

    z_waiting = {}

    def z_collect(i):
        copy = z_waiting.pop(i)
        copy.wait_recv()
        m = RZ_MOVES[i]
        GJ[J_INDEX[(m[3], 0)] - 15, :, half(m[2])] += RJ[i]

    def join(d):
        if d in shared:
            shared.pop(d).wait_recv()
            GJ[J_INDEX[(d, 0)] - 15] += RS[d]

    def send_z(i):
        m = RZ_MOVES[i]
        join(m[1])
        for f in RZ_FEEDS[i]:
            if f in z_waiting:
                z_collect(f)
        z_waiting[i] = push(m[0], GJ.at[J_INDEX[(m[1], 0)] - 15, :, half(m[2])], RJ.at[i])

    order = [(R_SLOT[i], 0, i) for i in range(len(R_MOVES))]
    z_slot = {"Z+": 1, "Z-": 1}
    for i, m in enumerate(RZ_MOVES):
        order.append((z_slot[m[0]], 1, i))
        z_slot[m[0]] += 2
    for _, kind, i in sorted(order):
        (send_z if kind else send_xy)(i)
    join(0)
    for i in sorted(waiting):
        collect(i)
    for i in sorted(z_waiting):
        z_collect(i)
    factor = 4.0 / jnp.sqrt(jnp.float32(TEXTS))
    out[:, :WI] = factor * GI[I_INDEX[(0, 0)]]
    out[:, WI:] = factor * GJ[0]
    for copy in copies:
        copy.wait_send()


COPIES = 1 + len(MOVES) + 2 * len(Z_MOVES) + 8 + len(R_MOVES) + len(RZ_MOVES)


def per_device(student, teacher, scales):
    return pl.pallas_call(
        kernel,
        out_shape=jax.ShapeDtypeStruct((ROWS, DS), jnp.float32),
        in_specs=[
            pl.BlockSpec(memory_space=pl.ANY),
            pl.BlockSpec(memory_space=pl.ANY),
            pl.BlockSpec(memory_space=pltpu.VMEM),
        ],
        out_specs=pl.BlockSpec(memory_space=pltpu.VMEM),
        scratch_shapes=[
            pltpu.VMEM((BLOCKS, ROWS, WIDTH), jnp.bfloat16),
            pltpu.VMEM((4, 4, GROUP, 256), jnp.float32),
            pltpu.VMEM((4, 4, GROUP, 256), jnp.bfloat16),
            pltpu.VMEM((16, ROWS, WI), jnp.float32),
            pltpu.VMEM((16, ROWS, WJ), jnp.float32),
            pltpu.VMEM((len(R_MOVES), ROWS, QI), jnp.float32),
            pltpu.VMEM((len(RZ_MOVES), ROWS, HJ), jnp.float32),
            pltpu.VMEM((8, ROWS, WJ), jnp.float32),
            pltpu.SemaphoreType.DMA((2,)),
            pltpu.SemaphoreType.DMA((COPIES,)),
            pltpu.SemaphoreType.DMA((COPIES,)),
        ],
        compiler_params=pltpu.CompilerParams(
            collective_id=0, has_side_effects=True, vmem_limit_bytes=56 * 2**20
        ),
        cost_estimate=pl.CostEstimate(flops=10**10, bytes_accessed=10**6, transcendentals=0),
        name="huber_gram",
    )(student, teacher, scales.reshape(1, ROWS))


def solution(mesh):
    return jax.shard_map(
        per_device,
        mesh=mesh,
        in_specs=(P(("row", "col"), None), P(("row", "col"), None), P(("row", "col"))),
        out_specs=P(("row", "col"), None),
        check_vma=False,
    )
```

```python
import functools
import jax
import jax.numpy as jnp
from jax import lax
from jax.experimental import pallas as pl
from jax.experimental.pallas import tpu as pltpu
from jax.sharding import PartitionSpec as P

DS, DT, ROWS, EXT = 1024, 4096, 56, 128
TEXTS = 14336
WIDTH = DT + DS + EXT
PIECES = ((0, 1280), (1280, 2560), (2560, 3840), (3840, WIDTH))
T_PIECES = ((0, 1280), (1280, 2560), (2560, 3840), (3840, DT))
LINKS = ("X+", "X-", "Y+", "Y-", "Z+", "Z-", "S")
GROUP = 4 * ROWS
WI = 512
WJ = DS - WI
QI, HJ = WI // 4, WJ // 4
LAG = 3
BUDGET = 2.2
HOP = 2.2
S_HOP = 2.5


def moved(block, link):
    step = 1 if link[1] == "+" else -1
    if link[0] == "X":
        return ((block[0] - step) % 4, block[1])
    return (block[0], (block[1] - step) % 4)


def gather_xy():
    out = []

    def ring(axis, heads, p, q):
        for head in heads:
            for link, far, order in ((axis + "+", p, (p, q)), (axis + "-", q, (q, p))):
                near = moved(head, link)
                out.extend((link, head, piece, near) for piece in order)
                out.append((link, near, far, moved(near, link)))

    ring("X", [(0, 0)], 0, 1)
    ring("Y", [(d, 0) for d in (2, 1, 3, 0)], 0, 1)
    ring("Y", [(0, 0)], 2, 3)
    ring("X", [(0, d) for d in (2, 1, 3, 0)], 2, 3)
    return out


def slots_of(moves, feeds, links, lag):
    n = len(moves)
    users = [[j for j in range(n) if i in feeds[j]] for i in range(n)]

    @functools.cache
    def height(i):
        return 1 + max([height(j) for j in users[i]], default=0)

    slot, now = {}, 0
    while len(slot) < n:
        now += 1
        for link in links:
            ready = [
                i for i in range(n)
                if i not in slot and moves[i][0] == link
                and all(f in slot and slot[f] + lag <= now for f in feeds[i])
            ]
            if ready:
                best = min(ready, key=lambda i: (-height(i), -len(users[i]), not {moves[i][3][0], moves[i][3][1]} & {2}, i))
                slot[best] = now
    return slot


def plan_gather():
    moves = gather_xy()
    source = {(m[3], m[2]): i for i, m in enumerate(moves)}
    feeds = [[source[(m[1], m[2])]] if (m[1], m[2]) in source else [] for m in moves]
    slot = slots_of(moves, feeds, LINKS[:4], LAG)
    return moves, feeds, slot


MOVES, FEEDS, SLOT = plan_gather()
LAST = max(SLOT.values())
ARRIVE = {}
for _i, _m in enumerate(MOVES):
    ARRIVE.setdefault(_m[3], {})[_m[2]] = SLOT[_i]
ARRIVE[(0, 0)] = {p: 0 for p in range(4)}
I_ORDER = sorted(ARRIVE, key=lambda b: (max(ARRIVE[b].values()), sum(ARRIVE[b].values()), b))
I_INDEX = {b: i for i, b in enumerate(I_ORDER)}
J_ORDER = [(0, 0), (0, 1), (4, 0), (4, 1)]
for _d in (1, 2, 3):
    J_ORDER += [(_d, 0), (8 - _d, 0), (_d, 1), (8 - _d, 1)]
J_INDEX = {b: 16 + i for i, b in enumerate(J_ORDER)}
OWN, OWN_J = I_INDEX[(0, 0)], J_INDEX[(0, 0)]
BLOCKS = 32

Z_MOVES = []
for _s in range(14):
    _d, _p = _s // 4, _s % 4
    Z_MOVES.append(("Z+", (8 - _d) % 8, _p, 7 - _d, _s + 1))
    Z_MOVES.append(("Z-", _d, (_p + 2) % 4, _d + 1, _s + 1))
J_ARRIVE = {b: {p: 0 for p in range(4)} for b in J_ORDER}
for _m in Z_MOVES:
    J_ARRIVE[(_m[3], 0)][_m[2]] = _m[4]
    J_ARRIVE[(_m[3], 1)][_m[2]] = _m[4] + 1


FIRST = {(0, 0), (1, 0), (2, 0)}


def plan_compute():
    i_at = [[max(ARRIVE[b][p] for b in I_ORDER[4 * g:4 * g + 4]) for p in range(4)] for g in range(4)]
    j_at = [[max(J_ARRIVE[b][p] for b in J_ORDER[4 * g:4 * g + 4]) for p in range(4)] for g in range(4)]
    left = {(i, j): [0, 1, 2, 3] for i in range(4) for j in range(4)}
    started = set()
    done = {i: 0 for i in range(4)}
    out = {}

    def runs(pieces):
        ranges = []
        for p in pieces:
            if ranges and ranges[-1][1] == T_PIECES[p][0]:
                ranges[-1][1] = T_PIECES[p][1]
            else:
                ranges.append(list(T_PIECES[p]))
        return ranges

    def pick(seen, budget, least, j_seen=None, only=None):
        cost, tasks = 0.0, []
        while cost < budget:
            best = None
            for i, j in sorted(left if only is None else only & set(left)):
                ready = [p for p in left[(i, j)] if i_at[i][p] <= seen and j_at[j][p] <= (j_seen or seen)]
                final = len(ready) == len(left[(i, j)])
                ready = ready if final else [p for p in ready if p != 3]
                if final or len(ready) >= least:
                    key = (final, len(ready), -i)
                    if best is None or key > best[0]:
                        best = (key, i, j, ready, final)
            if best is None:
                break
            _, i, j, ready, final = best
            cost += 0.14 * len(ready) + (0.15 if final else 0.02)
            tasks.append(("final" if final else "acc", i, j, runs(ready), (i, j) in started))
            started.add((i, j))
            left[(i, j)] = [p for p in left[(i, j)] if p not in ready]
            if final:
                del left[(i, j)]
                done[i] += 1
                if done[i] == 4:
                    tasks.append(("grad", i))
                    cost += 0.3
        return tasks, cost

    for now in range(1, LAST + 1):
        out[now], _ = pick(now - LAG, BUDGET, 1 if now > LAST - 5 else 2)
    for stage in range(LAST - LAG + 1, LAST):
        out["after", stage], _ = pick(stage, 9.0, 1, None, FIRST if stage == LAST - 1 else None)
    out["after", LAST], _ = pick(LAST - 1, 9.0, 1, LAST, FIRST)
    for j in (0, 3, 2, 1):
        tasks = []
        for i in range(4):
            if (i, j) in left:
                tasks.append(("final", i, j, runs(left.pop((i, j))), (i, j) in started))
                done[i] += 1
        out["last", j] = tasks
    assert not left
    out["late"] = [i for i in range(4) if ("grad", i) not in sum((v for v in out.values() if isinstance(v, list)), [])]
    return out


TASKS = plan_compute()


def plan_reduce():
    moves = []

    def ring(axis, heads, p, q):
        def at(head, d):
            return ((head[0] + d) % 4, head[1]) if axis == "X" else (head[0], (head[1] + d) % 4)
        for head in heads:
            plus, minus = axis + "+", axis + "-"
            moves.append((plus, at(head, 2), p, at(head, 1)))
            moves.append((minus, at(head, 2), q, at(head, 3)))
            for piece in (q, p):
                moves.append((plus, at(head, 1), piece, head))
            for piece in (p, q):
                moves.append((minus, at(head, 3), piece, head))

    ring("Y", [(d, 0) for d in (2, 1, 3, 0)], 0, 1)
    ring("X", [(0, 0)], 0, 1)
    ring("X", [(0, d) for d in (2, 1, 3, 0)], 2, 3)
    ring("Y", [(0, 0)], 2, 3)
    feeds = [[j for j, f in enumerate(moves) if f[3] == m[1] and f[2] == m[2]] for m in moves]
    return moves, feeds


R_MOVES, R_FEEDS = plan_reduce()
RZ_MOVES = []
for _d in (4, 3, 2, 1):
    for _q in (0, 1):
        RZ_MOVES.append(("Z+", _d, _q, _d - 1))
        RZ_MOVES.append(("Z-", (8 - _d) % 8, 2 + _q, (9 - _d) % 8))
    for _q in (0, 1):
        if _d < 4:
            RZ_MOVES.append(("Z+", _d, 2 + _q, _d - 1))
            RZ_MOVES.append(("Z-", (8 - _d) % 8, _q, (9 - _d) % 8))
RZ_FEEDS = [[j for j, f in enumerate(RZ_MOVES) if f[3] == m[1] and f[2] == m[2]] for m in RZ_MOVES]


def timed(moves, feeds, ready, length):
    n = len(moves)
    users = [[j for j in range(n) if i in feeds[j]] for i in range(n)]

    @functools.cache
    def height(i):
        return 1 + max([height(j) for j in users[i]], default=0)

    start, free = {}, {}
    while len(start) < n:
        best = None
        for i in range(n):
            if i in start or any(f not in start for f in feeds[i]):
                continue
            at = max([ready[i], free.get(moves[i][0], -9.0)] + [start[f] + length[i] + HOP for f in feeds[i]])
            key = (at, -height(i), i)
            if best is None or key < best:
                best = key
        at, _, i = best
        start[i] = at
        free[moves[i][0]] = at + length[i]
    return start


def dot(a, b, dims):
    return lax.dot_general(a, b, ((dims[0], dims[1]), ((), ())), preferred_element_type=jnp.float32)


def kernel(student, teacher, scales, out, X, acc, D, GI, GJ, RI, RJ, RS, load_sem, send, recv):
    row, col = lax.axis_index("row"), lax.axis_index("col")
    z, c = row // 2, row % 2
    x, y = col // 4, col % 4
    peer = {
        "X+": (row, ((x + 1) % 4) * 4 + y), "X-": (row, ((x + 3) % 4) * 4 + y),
        "Y+": (row, x * 4 + (y + 1) % 4), "Y-": (row, x * 4 + (y + 3) % 4),
        "Z+": (((z + 1) % 8) * 2 + c, col), "Z-": (((z + 7) % 8) * 2 + c, col),
        "S": (z * 2 + 1 - c, col),
    }
    loads = [
        pltpu.make_async_copy(teacher, X.at[OWN, :, pl.ds(0, DT)], load_sem.at[0]),
        pltpu.make_async_copy(student, X.at[OWN, :, pl.ds(DT, DS)], load_sem.at[1]),
        pltpu.make_async_copy(teacher, X.at[OWN_J, :, pl.ds(0, DT)], load_sem.at[2]),
        pltpu.make_async_copy(student, X.at[OWN_J, :, pl.ds(DT, DS)], load_sem.at[3]),
    ]
    for load in loads:
        load.start()
    barrier = pltpu.get_barrier_semaphore()
    for link in LINKS:
        pl.semaphore_signal(barrier, inc=1, device_id=peer[link], device_id_type=pl.DeviceIdType.MESH)
    here = lax.broadcasted_iota(jnp.int32, (ROWS, ROWS), 0) == lax.broadcasted_iota(jnp.int32, (ROWS, ROWS), 1)
    scale = jnp.sum(jnp.where(here, jnp.broadcast_to(scales[...], (ROWS, ROWS)), 0.0), axis=1, keepdims=True)
    high = scale.astype(jnp.bfloat16).astype(jnp.float32)
    mid = (scale - high).astype(jnp.bfloat16).astype(jnp.float32)
    low = scale - high - mid
    lane = lax.broadcasted_iota(jnp.int32, (ROWS, EXT), 1)
    terms = jnp.where(lane == 0, high, jnp.where(lane == 1, mid, jnp.where(lane == 2, low, 0.0)))
    X[OWN, :, DT + DS:] = terms.astype(jnp.bfloat16)
    X[OWN_J, :, DT + DS:] = terms.astype(jnp.bfloat16)
    for load in loads:
        load.wait()
    pl.semaphore_wait(barrier, len(LINKS))

    copies = []

    def push(link, src, dst):
        n = len(copies)
        copy = pltpu.make_async_remote_copy(
            src_ref=src, dst_ref=dst, send_sem=send.at[n], recv_sem=recv.at[n],
            device_id=peer[link], device_id_type=pl.DeviceIdType.MESH,
        )
        copy.start()
        copies.append(copy)
        return copy

    def part(index, piece):
        low_col, high_col = PIECES[piece]
        return X.at[index, :, pl.ds(low_col, high_col - low_col)]

    def i_rows(g, a, b):
        return X[4 * g:4 * g + 4, :, a:b].reshape(GROUP, b - a)

    def j_rows(g, a, b):
        return X[16 + 4 * g:20 + 4 * g, :, a:b].reshape(GROUP, b - a)

    def grad_i(i):
        total = None
        for j in range(4):
            term = dot(D[i, j, :, :GROUP], j_rows(j, DT, DT + WI), ((1,), (0,)))
            total = term if total is None else total + term
        for q in range(4):
            GI[q, 4 * i:4 * i + 4] = total[:, q * QI:(q + 1) * QI].reshape(4, ROWS, QI)

    def grad_j(j):
        total = None
        for i in range(4):
            term = dot(D[i, j, :, :GROUP], i_rows(i, DT + WI, DT + DS), ((0,), (0,)))
            total = term if total is None else total + term
        for h in range(4):
            GJ[h, 4 * j:4 * j + 4] = total[:, h * HJ:(h + 1) * HJ].reshape(4, ROWS, HJ)

    def run(task):
        kind, i = task[:2]
        if kind == "grad":
            grad_i(i)
            return
        j, ranges, started = task[2:]
        total = acc[i, j, :, :GROUP] if started else None
        for a, b in ranges:
            term = dot(i_rows(i, a, b), j_rows(j, a, b), ((1,), (1,)))
            total = term if total is None else total + term
        if kind == "acc":
            acc[i, j, :, :GROUP] = total
            return
        own = jnp.sum(i_rows(i, DT + DS, WIDTH).astype(jnp.float32), axis=1, keepdims=True)
        ones = jnp.ones((8, EXT), jnp.bfloat16)
        other = dot(ones, j_rows(j, DT + DS, WIDTH), ((1,), (1,)))[0:1]
        student_gram = dot(i_rows(i, DT, DT + DS), j_rows(j, DT, DT + DS), ((1,), (1,)))
        d = jnp.clip(student_gram - total * own * other, -0.25, 0.25)
        D[i, j, :, :GROUP] = d.astype(jnp.bfloat16)

    arriving, forwards = {}, {}
    first = push("S", X.at[OWN_J], X.at[J_INDEX[(0, 1)]])

    def wait_slot(s):
        if s == 0:
            first.wait_recv()
        for copy in forwards.pop(s - 1, []):
            copy.wait_recv()
        for copy in arriving.pop(("xy", s), []):
            copy.wait_recv()
        for copy, m in arriving.pop(("z", s), []):
            copy.wait_recv()
            forwards.setdefault(s, []).append(
                push("S", part(J_INDEX[(m[3], 0)], m[2]), part(J_INDEX[(m[3], 1)], m[2]))
            )

    for now in range(1, LAST + 1):
        if now > LAG - 1:
            wait_slot(now - LAG)
        for i, m in enumerate(MOVES):
            if SLOT[i] == now:
                copy = push(m[0], part(I_INDEX[m[1]], m[2]), part(I_INDEX[m[3]], m[2]))
                arriving.setdefault(("xy", now), []).append(copy)
        for m in Z_MOVES:
            if m[4] == now:
                copy = push(m[0], part(J_INDEX[(m[1], 0)], m[2]), part(J_INDEX[(m[3], 0)], m[2]))
                arriving.setdefault(("z", now), []).append((copy, m))
        for task in TASKS[now]:
            run(task)
    for stage in range(LAST - LAG + 1, LAST):
        wait_slot(stage)
        for task in TASKS["after", stage]:
            run(task)
    for copy in forwards.pop(LAST - 1, []):
        copy.wait_recv()
    for task in TASKS["after", LAST]:
        run(task)
    shared, waiting, z_waiting = {}, {}, {}

    def last(j):
        for task in TASKS["last", j]:
            run(task)
        grad_j(j)
        for d, core in reversed(J_ORDER[4 * j:4 * j + 4]):
            if core == 1:
                shared[d] = push("S", GJ.at[:, J_INDEX[(d, 1)] - 16], RS.at[d])

    def collect(i):
        if i not in waiting:
            return
        waiting.pop(i).wait_recv()
        m = R_MOVES[i]
        GI[m[2], I_INDEX[m[3]]] += RI[i]

    def send_xy(i):
        m = R_MOVES[i]
        for f in R_FEEDS[i]:
            if f in waiting:
                collect(f)
        waiting[i] = push(m[0], GI.at[m[2], I_INDEX[m[1]]], RI.at[i])

    def z_collect(i):
        if i not in z_waiting:
            return
        z_waiting.pop(i).wait_recv()
        m = RZ_MOVES[i]
        GJ[m[2], J_INDEX[(m[3], 0)] - 16] += RJ[i]

    def join(d):
        if d in shared:
            shared.pop(d).wait_recv()
            GJ[:, J_INDEX[(d, 0)] - 16] += RS[d]

    def send_z(i):
        m = RZ_MOVES[i]
        join(m[1])
        for f in RZ_FEEDS[i]:
            if f in z_waiting:
                z_collect(f)
        z_waiting[i] = push(m[0], GJ.at[m[2], J_INDEX[(m[1], 0)] - 16], RJ.at[i])

    steps, clock, j_ready, i_ready = [(-0.1, 0, wait_slot, LAST)], 0.0, {}, [-1.0] * 4
    for n, j in enumerate((0, 3, 2, 1)):
        steps.append((clock, n, last, j))
        clock += 0.3 + 0.75 * len(TASKS["last", j])
        for d, core in J_ORDER[4 * j:4 * j + 4]:
            j_ready[d] = clock + S_HOP
    for i in TASKS["late"]:
        steps.append((clock, 4 + i, grad_i, i))
        clock += 0.3
        i_ready[i] = clock
    starts = timed(R_MOVES, R_FEEDS, [i_ready[I_INDEX[m[1]] // 4] for m in R_MOVES], [0.62] * len(R_MOVES))
    for i, at in starts.items():
        steps.append((at, 10 + i, send_xy, i))
        got = max(at + 0.62 + HOP, i_ready[I_INDEX[R_MOVES[i][3]] // 4])
        steps.append((got, 200 + i, collect, i))
    starts = timed(RZ_MOVES, RZ_FEEDS, [j_ready[m[1]] for m in RZ_MOVES], [0.62] * len(RZ_MOVES))
    for i, at in starts.items():
        steps.append((at, 100 + i, send_z, i))
        got = max(at + 0.62 + HOP, j_ready[RZ_MOVES[i][3]])
        steps.append((got, 300 + i, z_collect, i))
    for _, _, act, what in sorted(steps, key=lambda step: step[:2]):
        act(what)
    assert not arriving and not forwards
    join(0)
    factor = 4.0 / jnp.sqrt(jnp.float32(TEXTS))
    for q in range(4):
        out[:, q * QI:(q + 1) * QI] = factor * GI[q, I_INDEX[(0, 0)]]
    for h in range(4):
        out[:, WI + h * HJ:WI + (h + 1) * HJ] = factor * GJ[h, 0]
    for copy in copies:
        copy.wait_send()


COPIES = 1 + len(MOVES) + 2 * len(Z_MOVES) + 8 + len(R_MOVES) + len(RZ_MOVES)


def per_device(student, teacher, scales):
    return pl.pallas_call(
        kernel,
        out_shape=jax.ShapeDtypeStruct((ROWS, DS), jnp.float32),
        in_specs=[
            pl.BlockSpec(memory_space=pl.ANY),
            pl.BlockSpec(memory_space=pl.ANY),
            pl.BlockSpec(memory_space=pltpu.VMEM),
        ],
        out_specs=pl.BlockSpec(memory_space=pltpu.VMEM),
        scratch_shapes=[
            pltpu.VMEM((BLOCKS, ROWS, WIDTH), jnp.bfloat16),
            pltpu.VMEM((4, 4, GROUP, 256), jnp.float32),
            pltpu.VMEM((4, 4, GROUP, 256), jnp.bfloat16),
            pltpu.VMEM((4, 16, ROWS, QI), jnp.float32),
            pltpu.VMEM((4, 16, ROWS, HJ), jnp.float32),
            pltpu.VMEM((len(R_MOVES), ROWS, QI), jnp.float32),
            pltpu.VMEM((len(RZ_MOVES), ROWS, HJ), jnp.float32),
            pltpu.VMEM((8, 4, ROWS, HJ), jnp.float32),
            pltpu.SemaphoreType.DMA((4,)),
            pltpu.SemaphoreType.DMA((COPIES,)),
            pltpu.SemaphoreType.DMA((COPIES,)),
        ],
        compiler_params=pltpu.CompilerParams(
            collective_id=0, has_side_effects=True, vmem_limit_bytes=56 * 2**20
        ),
        cost_estimate=pl.CostEstimate(flops=10**10, bytes_accessed=10**6, transcendentals=0),
        name="huber_gram",
    )(student, teacher, scales.reshape(1, ROWS))


def solution(mesh):
    return jax.shard_map(
        per_device,
        mesh=mesh,
        in_specs=(P(("row", "col"), None), P(("row", "col"), None), P(("row", "col"))),
        out_specs=P(("row", "col"), None),
        check_vma=False,
    )
```

```python
import functools
import jax
import jax.numpy as jnp
from jax import lax
from jax.experimental import pallas as pl
from jax.experimental.pallas import tpu as pltpu
from jax.sharding import PartitionSpec as P

DS, DT, ROWS, LANES = 1024, 4096, 56, 128
TEXTS = 14336
WIDTH = DT + DS
PIECES = ((0, 1280), (1280, 2560), (2560, 3840), (3840, WIDTH))
T_PIECES = ((0, 1280), (1280, 2560), (2560, 3840), (3840, DT))
LINKS = ("X+", "X-", "Y+", "Y-", "Z+", "Z-", "S")
GROUP = 4 * ROWS
WI = 512
WJ = DS - WI
QI, HJ = WI // 4, WJ // 4
LAG = 3
BUDGET = 2.2
HOP = 2.2
S_HOP = 2.5


def moved(block, link):
    step = 1 if link[1] == "+" else -1
    if link[0] == "X":
        return ((block[0] - step) % 4, block[1])
    return (block[0], (block[1] - step) % 4)


def gather_xy():
    out = []

    def ring(axis, heads, p, q):
        for head in heads:
            for link, far, order in ((axis + "+", p, (p, q)), (axis + "-", q, (q, p))):
                near = moved(head, link)
                out.extend((link, head, piece, near) for piece in order)
                out.append((link, near, far, moved(near, link)))

    ring("X", [(0, 0)], 0, 1)
    ring("Y", [(d, 0) for d in (2, 1, 3, 0)], 0, 1)
    ring("Y", [(0, 0)], 2, 3)
    ring("X", [(0, d) for d in (2, 1, 3, 0)], 2, 3)
    return out


def slots_of(moves, feeds, links, lag):
    n = len(moves)
    users = [[j for j in range(n) if i in feeds[j]] for i in range(n)]

    @functools.cache
    def height(i):
        return 1 + max([height(j) for j in users[i]], default=0)

    slot, now = {}, 0
    while len(slot) < n:
        now += 1
        for link in links:
            ready = [
                i for i in range(n)
                if i not in slot and moves[i][0] == link
                and all(f in slot and slot[f] + lag <= now for f in feeds[i])
            ]
            if ready:
                best = min(ready, key=lambda i: (-height(i), -len(users[i]), not {moves[i][3][0], moves[i][3][1]} & {2}, i))
                slot[best] = now
    return slot


def plan_gather():
    moves = gather_xy()
    source = {(m[3], m[2]): i for i, m in enumerate(moves)}
    feeds = [[source[(m[1], m[2])]] if (m[1], m[2]) in source else [] for m in moves]
    slot = slots_of(moves, feeds, LINKS[:4], LAG)
    return moves, feeds, slot


MOVES, FEEDS, SLOT = plan_gather()
LAST = max(SLOT.values())
ARRIVE = {}
for _i, _m in enumerate(MOVES):
    ARRIVE.setdefault(_m[3], {})[_m[2]] = SLOT[_i]
ARRIVE[(0, 0)] = {p: 0 for p in range(4)}
I_ORDER = sorted(ARRIVE, key=lambda b: (max(ARRIVE[b].values()), sum(ARRIVE[b].values()), b))
I_INDEX = {b: i for i, b in enumerate(I_ORDER)}
J_ORDER = [(0, 0), (0, 1), (4, 0), (4, 1)]
for _d in (1, 2, 3):
    J_ORDER += [(_d, 0), (8 - _d, 0), (_d, 1), (8 - _d, 1)]
J_INDEX = {b: 16 + i for i, b in enumerate(J_ORDER)}
OWN, OWN_J = I_INDEX[(0, 0)], J_INDEX[(0, 0)]
BLOCKS = 32

Z_MOVES = []
for _s in range(14):
    _d, _p = _s // 4, _s % 4
    Z_MOVES.append(("Z+", (8 - _d) % 8, _p, 7 - _d, _s + 1))
    Z_MOVES.append(("Z-", _d, (_p + 2) % 4, _d + 1, _s + 1))
J_ARRIVE = {b: {p: 0 for p in range(4)} for b in J_ORDER}
for _m in Z_MOVES:
    J_ARRIVE[(_m[3], 0)][_m[2]] = _m[4]
    J_ARRIVE[(_m[3], 1)][_m[2]] = _m[4] + 1


FIRST = {(0, 0), (1, 0), (2, 0)}


def plan_compute():
    i_at = [[max(ARRIVE[b][p] for b in I_ORDER[4 * g:4 * g + 4]) for p in range(4)] for g in range(4)]
    j_at = [[max(J_ARRIVE[b][p] for b in J_ORDER[4 * g:4 * g + 4]) for p in range(4)] for g in range(4)]
    left = {(i, j): [0, 1, 2, 3] for i in range(4) for j in range(4)}
    started = set()
    done = {i: 0 for i in range(4)}
    out = {}

    def runs(pieces):
        ranges = []
        for p in pieces:
            if ranges and ranges[-1][1] == T_PIECES[p][0]:
                ranges[-1][1] = T_PIECES[p][1]
            else:
                ranges.append(list(T_PIECES[p]))
        return ranges

    def pick(seen, budget, least, j_seen=None, only=None):
        cost, tasks = 0.0, []
        while cost < budget:
            best = None
            for i, j in sorted(left if only is None else only & set(left)):
                ready = [p for p in left[(i, j)] if i_at[i][p] <= seen and j_at[j][p] <= (j_seen or seen)]
                final = len(ready) == len(left[(i, j)])
                ready = ready if final else [p for p in ready if p != 3]
                if final or len(ready) >= least:
                    key = (final, len(ready), -i)
                    if best is None or key > best[0]:
                        best = (key, i, j, ready, final)
            if best is None:
                break
            _, i, j, ready, final = best
            cost += 0.14 * len(ready) + (0.15 if final else 0.02)
            tasks.append(("final" if final else "acc", i, j, runs(ready), (i, j) in started))
            started.add((i, j))
            left[(i, j)] = [p for p in left[(i, j)] if p not in ready]
            if final:
                del left[(i, j)]
                done[i] += 1
                if done[i] == 4:
                    tasks.append(("grad", i))
                    cost += 0.3
        return tasks, cost

    for now in range(1, LAST + 1):
        out[now], _ = pick(now - LAG, BUDGET, 1 if now > LAST - 5 else 2)
    for stage in range(LAST - LAG + 1, LAST):
        out["after", stage], _ = pick(stage, 9.0, 1, None, FIRST if stage == LAST - 1 else None)
    out["after", LAST], _ = pick(LAST - 1, 9.0, 1, LAST, FIRST)
    for j in (0, 3, 2, 1):
        tasks = []
        for i in range(4):
            if (i, j) in left:
                tasks.append(("final", i, j, runs(left.pop((i, j))), (i, j) in started))
                done[i] += 1
        out["last", j] = tasks
    assert not left
    out["late"] = [i for i in range(4) if ("grad", i) not in sum((v for v in out.values() if isinstance(v, list)), [])]
    return out


TASKS = plan_compute()


def plan_reduce():
    moves = []

    def ring(axis, heads, p, q):
        def at(head, d):
            return ((head[0] + d) % 4, head[1]) if axis == "X" else (head[0], (head[1] + d) % 4)
        for head in heads:
            plus, minus = axis + "+", axis + "-"
            moves.append((plus, at(head, 2), p, at(head, 1)))
            moves.append((minus, at(head, 2), q, at(head, 3)))
            for piece in (q, p):
                moves.append((plus, at(head, 1), piece, head))
            for piece in (p, q):
                moves.append((minus, at(head, 3), piece, head))

    ring("Y", [(d, 0) for d in (2, 1, 3, 0)], 0, 1)
    ring("X", [(0, 0)], 0, 1)
    ring("X", [(0, d) for d in (2, 1, 3, 0)], 2, 3)
    ring("Y", [(0, 0)], 2, 3)
    feeds = [[j for j, f in enumerate(moves) if f[3] == m[1] and f[2] == m[2]] for m in moves]
    return moves, feeds


R_MOVES, R_FEEDS = plan_reduce()
RZ_MOVES = []
for _d in (4, 3, 2, 1):
    for _q in (0, 1):
        RZ_MOVES.append(("Z+", _d, _q, _d - 1))
        RZ_MOVES.append(("Z-", (8 - _d) % 8, 2 + _q, (9 - _d) % 8))
    for _q in (0, 1):
        if _d < 4:
            RZ_MOVES.append(("Z+", _d, 2 + _q, _d - 1))
            RZ_MOVES.append(("Z-", (8 - _d) % 8, _q, (9 - _d) % 8))
RZ_FEEDS = [[j for j, f in enumerate(RZ_MOVES) if f[3] == m[1] and f[2] == m[2]] for m in RZ_MOVES]


def timed(moves, feeds, ready, length):
    n = len(moves)
    users = [[j for j in range(n) if i in feeds[j]] for i in range(n)]

    @functools.cache
    def height(i):
        return 1 + max([height(j) for j in users[i]], default=0)

    start, free = {}, {}
    while len(start) < n:
        best = None
        for i in range(n):
            if i in start or any(f not in start for f in feeds[i]):
                continue
            at = max([ready[i], free.get(moves[i][0], -9.0)] + [start[f] + length[i] + HOP for f in feeds[i]])
            key = (at, -height(i), i)
            if best is None or key < best:
                best = key
        at, _, i = best
        start[i] = at
        free[moves[i][0]] = at + length[i]
    return start


def dot(a, b, dims):
    return lax.dot_general(a, b, ((dims[0], dims[1]), ((), ())), preferred_element_type=jnp.float32)


def kernel(student, teacher, scales, out, X, SC, SI, SJ, acc, D, GI, GJ, RI, RJ, RS, load_sem, send, recv):
    row, col = lax.axis_index("row"), lax.axis_index("col")
    z, c = row // 2, row % 2
    x, y = col // 4, col % 4
    peer = {
        "X+": (row, ((x + 1) % 4) * 4 + y), "X-": (row, ((x + 3) % 4) * 4 + y),
        "Y+": (row, x * 4 + (y + 1) % 4), "Y-": (row, x * 4 + (y + 3) % 4),
        "Z+": (((z + 1) % 8) * 2 + c, col), "Z-": (((z + 7) % 8) * 2 + c, col),
        "S": (z * 2 + 1 - c, col),
    }
    loads = [
        pltpu.make_async_copy(teacher, X.at[OWN, :, pl.ds(0, DT)], load_sem.at[0]),
        pltpu.make_async_copy(student, X.at[OWN, :, pl.ds(DT, DS)], load_sem.at[1]),
        pltpu.make_async_copy(teacher, X.at[OWN_J, :, pl.ds(0, DT)], load_sem.at[2]),
        pltpu.make_async_copy(student, X.at[OWN_J, :, pl.ds(DT, DS)], load_sem.at[3]),
    ]
    for load in loads:
        load.start()
    barrier = pltpu.get_barrier_semaphore()
    for link in LINKS:
        pl.semaphore_signal(barrier, inc=1, device_id=peer[link], device_id_type=pl.DeviceIdType.MESH)
    for own in (OWN, OWN_J):
        SC[own] = jnp.zeros((8, LANES), jnp.float32)
        SC[own, 0:1, 0:ROWS] = scales[...]
    for load in loads:
        load.wait()
    pl.semaphore_wait(barrier, len(LINKS))

    copies = []

    def push(link, src, dst):
        n = len(copies)
        copy = pltpu.make_async_remote_copy(
            src_ref=src, dst_ref=dst, send_sem=send.at[n], recv_sem=recv.at[n],
            device_id=peer[link], device_id_type=pl.DeviceIdType.MESH,
        )
        copy.start()
        copies.append(copy)
        return copy

    def part(index, piece):
        low_col, high_col = PIECES[piece]
        return X.at[index, :, pl.ds(low_col, high_col - low_col)]

    def push_part(link, src, dst, piece):
        out = [push(link, part(src, piece), part(dst, piece))]
        if piece == 3:
            out.append(push(link, SC.at[src], SC.at[dst]))
        return out

    def i_rows(g, a, b):
        return X[4 * g:4 * g + 4, :, a:b].reshape(GROUP, b - a)

    def j_rows(g, a, b):
        return X[16 + 4 * g:20 + 4 * g, :, a:b].reshape(GROUP, b - a)

    scaled = set()
    eye = lax.broadcasted_iota(jnp.int32, (ROWS, ROWS), 0) == lax.broadcasted_iota(jnp.int32, (ROWS, ROWS), 1)

    def grad_i(i):
        total = None
        for j in range(4):
            term = dot(D[i, j, :, :GROUP], j_rows(j, DT, DT + WI), ((1,), (0,)))
            total = term if total is None else total + term
        for q in range(4):
            GI[q, 4 * i:4 * i + 4] = total[:, q * QI:(q + 1) * QI].reshape(4, ROWS, QI)

    def grad_j(j):
        total = None
        for i in range(4):
            term = dot(D[i, j, :, :GROUP], i_rows(i, DT + WI, DT + DS), ((0,), (0,)))
            total = term if total is None else total + term
        for h in range(4):
            GJ[h, 4 * j:4 * j + 4] = total[:, h * HJ:(h + 1) * HJ].reshape(4, ROWS, HJ)

    def run(task):
        kind, i = task[:2]
        if kind == "grad":
            grad_i(i)
            return
        j, ranges, started = task[2:]
        total = acc[i, j, :, :GROUP] if started else None
        for a, b in ranges:
            term = dot(i_rows(i, a, b), j_rows(j, a, b), ((1,), (1,)))
            total = term if total is None else total + term
        if kind == "acc":
            acc[i, j, :, :GROUP] = total
            return
        if ("i", i) not in scaled:
            scaled.add(("i", i))
            for b in range(4 * i, 4 * i + 4):
                line = jnp.broadcast_to(SC[b, 0:1, 0:ROWS], (ROWS, ROWS))
                column = jnp.sum(jnp.where(eye, line, 0.0), axis=1, keepdims=True)
                SI[b] = jnp.broadcast_to(column, (ROWS, LANES))
        if ("j", j) not in scaled:
            scaled.add(("j", j))
            line = jnp.zeros((8, 2 * LANES), jnp.float32)
            for k in range(4):
                wide = jnp.concatenate([SC[16 + 4 * j + k], jnp.zeros((8, LANES), jnp.float32)], axis=1)
                line = line + (pltpu.roll(wide, ROWS * k, 1) if k else wide)
            SJ[j] = line
        own = SI[4 * i:4 * i + 4].reshape(GROUP, LANES)[:, 0:1]
        other = SJ[j, 0:1, 0:GROUP]
        student_gram = dot(i_rows(i, DT, DT + DS), j_rows(j, DT, DT + DS), ((1,), (1,)))
        d = jnp.clip(student_gram - total * own * other, -0.25, 0.25)
        D[i, j, :, :GROUP] = d.astype(jnp.bfloat16)

    arriving, forwards = {}, {}
    first = [
        push("S", X.at[OWN_J], X.at[J_INDEX[(0, 1)]]),
        push("S", SC.at[OWN_J], SC.at[J_INDEX[(0, 1)]]),
    ]

    def wait_slot(s):
        if s == 0:
            for copy in first:
                copy.wait_recv()
        for copy in forwards.pop(s - 1, []):
            copy.wait_recv()
        for copy in arriving.pop(("xy", s), []):
            copy.wait_recv()
        for copy, m in arriving.pop(("z", s), []):
            copy.wait_recv()
            if m is not None:
                forwards.setdefault(s, []).extend(
                    push_part("S", J_INDEX[(m[3], 0)], J_INDEX[(m[3], 1)], m[2])
                )

    for now in range(1, LAST + 1):
        if now > LAG - 1:
            wait_slot(now - LAG)
        for i, m in enumerate(MOVES):
            if SLOT[i] == now:
                arriving.setdefault(("xy", now), []).extend(
                    push_part(m[0], I_INDEX[m[1]], I_INDEX[m[3]], m[2])
                )
        for m in Z_MOVES:
            if m[4] == now:
                pair = push_part(m[0], J_INDEX[(m[1], 0)], J_INDEX[(m[3], 0)], m[2])
                arriving.setdefault(("z", now), []).extend((copy, m if copy is pair[-1] else None) for copy in pair)
        for task in TASKS[now]:
            run(task)
    for stage in range(LAST - LAG + 1, LAST):
        wait_slot(stage)
        for task in TASKS["after", stage]:
            run(task)
    for copy in forwards.pop(LAST - 1, []):
        copy.wait_recv()
    for task in TASKS["after", LAST]:
        run(task)
    shared, waiting, z_waiting = {}, {}, {}

    def last(j):
        for task in TASKS["last", j]:
            run(task)
        grad_j(j)
        for d, core in reversed(J_ORDER[4 * j:4 * j + 4]):
            if core == 1:
                shared[d] = push("S", GJ.at[:, J_INDEX[(d, 1)] - 16], RS.at[d])

    def collect(i):
        if i not in waiting:
            return
        waiting.pop(i).wait_recv()
        m = R_MOVES[i]
        GI[m[2], I_INDEX[m[3]]] += RI[i]

    def send_xy(i):
        m = R_MOVES[i]
        for f in R_FEEDS[i]:
            if f in waiting:
                collect(f)
        waiting[i] = push(m[0], GI.at[m[2], I_INDEX[m[1]]], RI.at[i])

    def z_collect(i):
        if i not in z_waiting:
            return
        z_waiting.pop(i).wait_recv()
        m = RZ_MOVES[i]
        GJ[m[2], J_INDEX[(m[3], 0)] - 16] += RJ[i]

    def join(d):
        if d in shared:
            shared.pop(d).wait_recv()
            GJ[:, J_INDEX[(d, 0)] - 16] += RS[d]

    def send_z(i):
        m = RZ_MOVES[i]
        join(m[1])
        for f in RZ_FEEDS[i]:
            if f in z_waiting:
                z_collect(f)
        z_waiting[i] = push(m[0], GJ.at[m[2], J_INDEX[(m[1], 0)] - 16], RJ.at[i])

    steps, clock, j_ready, i_ready = [(-0.1, 0, wait_slot, LAST)], 0.0, {}, [-1.0] * 4
    for n, j in enumerate((0, 3, 2, 1)):
        steps.append((clock, n, last, j))
        clock += 0.3 + 0.75 * len(TASKS["last", j])
        for d, core in J_ORDER[4 * j:4 * j + 4]:
            j_ready[d] = clock + S_HOP
    for i in TASKS["late"]:
        steps.append((clock, 4 + i, grad_i, i))
        clock += 0.3
        i_ready[i] = clock
    starts = timed(R_MOVES, R_FEEDS, [i_ready[I_INDEX[m[1]] // 4] for m in R_MOVES], [0.62] * len(R_MOVES))
    for i, at in starts.items():
        steps.append((at, 10 + i, send_xy, i))
        got = max(at + 0.62 + HOP, i_ready[I_INDEX[R_MOVES[i][3]] // 4])
        steps.append((got, 200 + i, collect, i))
    starts = timed(RZ_MOVES, RZ_FEEDS, [j_ready[m[1]] for m in RZ_MOVES], [0.62] * len(RZ_MOVES))
    for i, at in starts.items():
        steps.append((at, 100 + i, send_z, i))
        got = max(at + 0.62 + HOP, j_ready[RZ_MOVES[i][3]])
        steps.append((got, 300 + i, z_collect, i))
    for _, _, act, what in sorted(steps, key=lambda step: step[:2]):
        act(what)
    assert not arriving and not forwards
    join(0)
    factor = 4.0 / jnp.sqrt(jnp.float32(TEXTS))
    for q in range(4):
        out[:, q * QI:(q + 1) * QI] = factor * GI[q, I_INDEX[(0, 0)]]
    for h in range(4):
        out[:, WI + h * HJ:WI + (h + 1) * HJ] = factor * GJ[h, 0]
    for copy in copies:
        copy.wait_send()


COPIES = 32 + len(MOVES) + 2 * len(Z_MOVES) + 8 + len(R_MOVES) + len(RZ_MOVES)


def per_device(student, teacher, scales):
    return pl.pallas_call(
        kernel,
        out_shape=jax.ShapeDtypeStruct((ROWS, DS), jnp.float32),
        in_specs=[
            pl.BlockSpec(memory_space=pl.ANY),
            pl.BlockSpec(memory_space=pl.ANY),
            pl.BlockSpec(memory_space=pltpu.VMEM),
        ],
        out_specs=pl.BlockSpec(memory_space=pltpu.VMEM),
        scratch_shapes=[
            pltpu.VMEM((BLOCKS, ROWS, WIDTH), jnp.bfloat16),
            pltpu.VMEM((BLOCKS, 8, LANES), jnp.float32),
            pltpu.VMEM((16, ROWS, LANES), jnp.float32),
            pltpu.VMEM((4, 8, 2 * LANES), jnp.float32),
            pltpu.VMEM((4, 4, GROUP, 256), jnp.float32),
            pltpu.VMEM((4, 4, GROUP, 256), jnp.bfloat16),
            pltpu.VMEM((4, 16, ROWS, QI), jnp.float32),
            pltpu.VMEM((4, 16, ROWS, HJ), jnp.float32),
            pltpu.VMEM((len(R_MOVES), ROWS, QI), jnp.float32),
            pltpu.VMEM((len(RZ_MOVES), ROWS, HJ), jnp.float32),
            pltpu.VMEM((8, 4, ROWS, HJ), jnp.float32),
            pltpu.SemaphoreType.DMA((4,)),
            pltpu.SemaphoreType.DMA((COPIES,)),
            pltpu.SemaphoreType.DMA((COPIES,)),
        ],
        compiler_params=pltpu.CompilerParams(
            collective_id=0, has_side_effects=True, vmem_limit_bytes=56 * 2**20
        ),
        cost_estimate=pl.CostEstimate(flops=10**10, bytes_accessed=10**6, transcendentals=0),
        name="huber_gram",
    )(student, teacher, scales.reshape(1, ROWS))


def solution(mesh):
    return jax.shard_map(
        per_device,
        mesh=mesh,
        in_specs=(P(("row", "col"), None), P(("row", "col"), None), P(("row", "col"))),
        out_specs=P(("row", "col"), None),
        check_vma=False,
    )
```

```python
import functools
import jax
import jax.numpy as jnp
from jax import lax
from jax.experimental import pallas as pl
from jax.experimental.pallas import tpu as pltpu
from jax.sharding import PartitionSpec as P

DS, DT, ROWS, LANES = 1024, 4096, 56, 128
TEXTS = 14336
WIDTH = DT + DS
PIECES = ((0, 1280), (1280, 2560), (2560, 3840), (3840, WIDTH))
T_PIECES = ((0, 1280), (1280, 2560), (2560, 3840), (3840, DT))
LINKS = ("X+", "X-", "Y+", "Y-", "Z+", "Z-", "S")
GROUP = 4 * ROWS
WI = 512
WJ = DS - WI
QI, HJ = WI // 4, WJ // 4
LAG = 3
BUDGET = 2.2
HOP = 2.2
S_HOP = 2.5


def moved(block, link):
    step = 1 if link[1] == "+" else -1
    if link[0] == "X":
        return ((block[0] - step) % 4, block[1])
    return (block[0], (block[1] - step) % 4)


def gather_xy():
    out = []

    def ring(axis, heads, p, q):
        for head in heads:
            for link, far, order in ((axis + "+", p, (p, q)), (axis + "-", q, (q, p))):
                near = moved(head, link)
                out.extend((link, head, piece, near) for piece in order)
                out.append((link, near, far, moved(near, link)))

    ring("X", [(0, 0)], 0, 1)
    ring("Y", [(d, 0) for d in (2, 1, 3, 0)], 0, 1)
    ring("Y", [(0, 0)], 2, 3)
    ring("X", [(0, d) for d in (2, 1, 3, 0)], 2, 3)
    return out


def slots_of(moves, feeds, links, lag):
    n = len(moves)
    users = [[j for j in range(n) if i in feeds[j]] for i in range(n)]

    @functools.cache
    def height(i):
        return 1 + max([height(j) for j in users[i]], default=0)

    slot, now = {}, 0
    while len(slot) < n:
        now += 1
        for link in links:
            ready = [
                i for i in range(n)
                if i not in slot and moves[i][0] == link
                and all(f in slot and slot[f] + lag <= now for f in feeds[i])
            ]
            if ready:
                best = min(ready, key=lambda i: (-height(i), -len(users[i]), not {moves[i][3][0], moves[i][3][1]} & {2}, i))
                slot[best] = now
    return slot


def plan_gather():
    moves = gather_xy()
    source = {(m[3], m[2]): i for i, m in enumerate(moves)}
    feeds = [[source[(m[1], m[2])]] if (m[1], m[2]) in source else [] for m in moves]
    slot = slots_of(moves, feeds, LINKS[:4], LAG)
    return moves, feeds, slot


MOVES, FEEDS, SLOT = plan_gather()
LAST = max(SLOT.values())
ARRIVE = {}
for _i, _m in enumerate(MOVES):
    ARRIVE.setdefault(_m[3], {})[_m[2]] = SLOT[_i]
ARRIVE[(0, 0)] = {p: 0 for p in range(4)}
I_ORDER = sorted(ARRIVE, key=lambda b: (max(ARRIVE[b].values()), sum(ARRIVE[b].values()), b))
I_INDEX = {b: i for i, b in enumerate(I_ORDER)}
J_ORDER = [(0, 0), (0, 1), (4, 0), (4, 1)]
for _d in (1, 2, 3):
    J_ORDER += [(_d, 0), (8 - _d, 0), (_d, 1), (8 - _d, 1)]
J_INDEX = {b: 16 + i for i, b in enumerate(J_ORDER)}
OWN, OWN_J = I_INDEX[(0, 0)], J_INDEX[(0, 0)]
BLOCKS = 32

Z_MOVES = []
for _s in range(14):
    _d, _p = _s // 4, _s % 4
    Z_MOVES.append(("Z+", (8 - _d) % 8, _p, 7 - _d, _s + 1))
    Z_MOVES.append(("Z-", _d, (_p + 2) % 4, _d + 1, _s + 1))
J_ARRIVE = {b: {p: 0 for p in range(4)} for b in J_ORDER}
for _m in Z_MOVES:
    J_ARRIVE[(_m[3], 0)][_m[2]] = _m[4]
    J_ARRIVE[(_m[3], 1)][_m[2]] = _m[4] + 1


FIRST = {(0, 0), (1, 0), (2, 0)}


def plan_compute():
    i_at = [[max(ARRIVE[b][p] for b in I_ORDER[4 * g:4 * g + 4]) for p in range(4)] for g in range(4)]
    j_at = [[max(J_ARRIVE[b][p] for b in J_ORDER[4 * g:4 * g + 4]) for p in range(4)] for g in range(4)]
    left = {(i, j): [0, 1, 2, 3] for i in range(4) for j in range(4)}
    started = set()
    done = {i: 0 for i in range(4)}
    out = {}

    def runs(pieces):
        ranges = []
        for p in pieces:
            if ranges and ranges[-1][1] == T_PIECES[p][0]:
                ranges[-1][1] = T_PIECES[p][1]
            else:
                ranges.append(list(T_PIECES[p]))
        return ranges

    def pick(seen, budget, least, j_seen=None, only=None):
        cost, tasks = 0.0, []
        while cost < budget:
            best = None
            for i, j in sorted(left if only is None else only & set(left)):
                ready = [p for p in left[(i, j)] if i_at[i][p] <= seen and j_at[j][p] <= (j_seen or seen)]
                final = len(ready) == len(left[(i, j)])
                ready = ready if final else [p for p in ready if p != 3]
                if final or len(ready) >= least:
                    key = (final, len(ready), -i)
                    if best is None or key > best[0]:
                        best = (key, i, j, ready, final)
            if best is None:
                break
            _, i, j, ready, final = best
            cost += 0.14 * len(ready) + (0.15 if final else 0.02)
            tasks.append(("final" if final else "acc", i, j, runs(ready), (i, j) in started))
            started.add((i, j))
            left[(i, j)] = [p for p in left[(i, j)] if p not in ready]
            if final:
                del left[(i, j)]
                done[i] += 1
                if done[i] == 4:
                    tasks.append(("grad", i))
                    cost += 0.3
        return tasks, cost

    for now in range(1, LAST + 1):
        out[now], _ = pick(now - LAG, BUDGET, 1 if now > LAST - 5 else 2)
    for stage in range(LAST - LAG + 1, LAST):
        out["after", stage], _ = pick(stage, 9.0, 1, None, FIRST if stage == LAST - 1 else None)
    out["after", LAST], _ = pick(LAST - 1, 9.0, 1, LAST, FIRST)
    for j in (0, 3, 2, 1):
        tasks = []
        for i in range(4):
            if (i, j) in left:
                tasks.append(("final", i, j, runs(left.pop((i, j))), (i, j) in started))
                done[i] += 1
        out["last", j] = tasks
    assert not left
    out["late"] = [i for i in range(4) if ("grad", i) not in sum((v for v in out.values() if isinstance(v, list)), [])]
    return out


TASKS = plan_compute()


def plan_reduce():
    moves = []

    def ring(axis, heads, p, q):
        def at(head, d):
            return ((head[0] + d) % 4, head[1]) if axis == "X" else (head[0], (head[1] + d) % 4)
        for head in heads:
            plus, minus = axis + "+", axis + "-"
            moves.append((plus, at(head, 2), p, at(head, 1)))
            moves.append((minus, at(head, 2), q, at(head, 3)))
            for piece in (q, p):
                moves.append((plus, at(head, 1), piece, head))
            for piece in (p, q):
                moves.append((minus, at(head, 3), piece, head))

    ring("Y", [(d, 0) for d in (2, 1, 3, 0)], 0, 1)
    ring("X", [(0, 0)], 0, 1)
    ring("X", [(0, d) for d in (2, 1, 3, 0)], 2, 3)
    ring("Y", [(0, 0)], 2, 3)
    feeds = [[j for j, f in enumerate(moves) if f[3] == m[1] and f[2] == m[2]] for m in moves]
    return moves, feeds


R_MOVES, R_FEEDS = plan_reduce()
RZ_MOVES = []
for _d in (4, 3, 2, 1):
    for _q in (0, 1):
        RZ_MOVES.append(("Z+", _d, _q, _d - 1))
        RZ_MOVES.append(("Z-", (8 - _d) % 8, 2 + _q, (9 - _d) % 8))
    for _q in (0, 1):
        if _d < 4:
            RZ_MOVES.append(("Z+", _d, 2 + _q, _d - 1))
            RZ_MOVES.append(("Z-", (8 - _d) % 8, _q, (9 - _d) % 8))
RZ_FEEDS = [[j for j, f in enumerate(RZ_MOVES) if f[3] == m[1] and f[2] == m[2]] for m in RZ_MOVES]


def timed(moves, feeds, ready, length):
    n = len(moves)
    users = [[j for j in range(n) if i in feeds[j]] for i in range(n)]

    @functools.cache
    def height(i):
        return 1 + max([height(j) for j in users[i]], default=0)

    start, free = {}, {}
    while len(start) < n:
        best = None
        for i in range(n):
            if i in start or any(f not in start for f in feeds[i]):
                continue
            at = max([ready[i], free.get(moves[i][0], -9.0)] + [start[f] + length[i] + HOP for f in feeds[i]])
            key = (at, -height(i), i)
            if best is None or key < best:
                best = key
        at, _, i = best
        start[i] = at
        free[moves[i][0]] = at + length[i]
    return start


def dot(a, b, dims):
    return lax.dot_general(a, b, ((dims[0], dims[1]), ((), ())), preferred_element_type=jnp.float32)


def kernel(student, teacher, scales, out, X, SC, SI, SJ, acc, D, GI, GJ, RI, RJ, RS, load_sem, send, recv):
    row, col = lax.axis_index("row"), lax.axis_index("col")
    z, c = row // 2, row % 2
    x, y = col // 4, col % 4
    peer = {
        "X+": (row, ((x + 1) % 4) * 4 + y), "X-": (row, ((x + 3) % 4) * 4 + y),
        "Y+": (row, x * 4 + (y + 1) % 4), "Y-": (row, x * 4 + (y + 3) % 4),
        "Z+": (((z + 1) % 8) * 2 + c, col), "Z-": (((z + 7) % 8) * 2 + c, col),
        "S": (z * 2 + 1 - c, col),
    }
    loads = [
        pltpu.make_async_copy(teacher, X.at[OWN, :, pl.ds(0, DT)], load_sem.at[0]),
        pltpu.make_async_copy(student, X.at[OWN, :, pl.ds(DT, DS)], load_sem.at[1]),
        pltpu.make_async_copy(teacher, X.at[OWN_J, :, pl.ds(0, DT)], load_sem.at[2]),
        pltpu.make_async_copy(student, X.at[OWN_J, :, pl.ds(DT, DS)], load_sem.at[3]),
    ]
    for load in loads:
        load.start()
    barrier = pltpu.get_barrier_semaphore()
    for link in LINKS:
        pl.semaphore_signal(barrier, inc=1, device_id=peer[link], device_id_type=pl.DeviceIdType.MESH)
    for own in (OWN, OWN_J):
        SC[own] = jnp.zeros((8, LANES), jnp.float32)
        SC[own, 0:1, 0:ROWS] = scales[...]
    for load in loads:
        load.wait()
    pl.semaphore_wait(barrier, len(LINKS))

    copies = []

    def push(link, src, dst):
        n = len(copies)
        copy = pltpu.make_async_remote_copy(
            src_ref=src, dst_ref=dst, send_sem=send.at[n], recv_sem=recv.at[n],
            device_id=peer[link], device_id_type=pl.DeviceIdType.MESH,
        )
        copy.start()
        copies.append(copy)
        return copy

    def part(index, piece):
        low_col, high_col = PIECES[piece]
        return X.at[index, :, pl.ds(low_col, high_col - low_col)]

    def push_part(link, src, dst, piece):
        out = [push(link, part(src, piece), part(dst, piece))]
        if piece == 3:
            out.append(push(link, SC.at[src], SC.at[dst]))
        return out

    def i_rows(g, a, b):
        return X[4 * g:4 * g + 4, :, a:b].reshape(GROUP, b - a)

    def j_rows(g, a, b):
        return X[16 + 4 * g:20 + 4 * g, :, a:b].reshape(GROUP, b - a)

    scaled = set()
    eye = lax.broadcasted_iota(jnp.int32, (ROWS, ROWS), 0) == lax.broadcasted_iota(jnp.int32, (ROWS, ROWS), 1)

    def grad_i(i):
        total = None
        for j in range(4):
            term = dot(D[i, j, :, :GROUP], j_rows(j, DT, DT + WI), ((1,), (0,)))
            total = term if total is None else total + term
        for q in range(4):
            GI[q, 4 * i:4 * i + 4] = total[:, q * QI:(q + 1) * QI].reshape(4, ROWS, QI)

    def grad_j(j):
        total = None
        for i in range(4):
            term = dot(D[i, j, :, :GROUP], i_rows(i, DT + WI, DT + DS), ((0,), (0,)))
            total = term if total is None else total + term
        for h in range(4):
            GJ[h, 4 * j:4 * j + 4] = total[:, h * HJ:(h + 1) * HJ].reshape(4, ROWS, HJ)

    def run(task):
        kind, i = task[:2]
        if kind == "grad":
            grad_i(i)
            return
        j, ranges, started = task[2:]
        total = acc[i, j, :, :GROUP] if started else None
        for a, b in ranges:
            term = dot(i_rows(i, a, b), j_rows(j, a, b), ((1,), (1,)))
            total = term if total is None else total + term
        if kind == "acc":
            acc[i, j, :, :GROUP] = total
            return
        if ("i", i) not in scaled:
            scaled.add(("i", i))
            for b in range(4 * i, 4 * i + 4):
                line = jnp.broadcast_to(SC[b, 0:1, 0:ROWS], (ROWS, ROWS))
                column = jnp.sum(jnp.where(eye, line, 0.0), axis=1, keepdims=True)
                SI[b] = jnp.broadcast_to(column, (ROWS, LANES))
        if ("j", j) not in scaled:
            scaled.add(("j", j))
            line = jnp.zeros((8, 2 * LANES), jnp.float32)
            for k in range(4):
                wide = jnp.concatenate([SC[16 + 4 * j + k], jnp.zeros((8, LANES), jnp.float32)], axis=1)
                line = line + (pltpu.roll(wide, ROWS * k, 1) if k else wide)
            SJ[j] = line
        own = SI[4 * i:4 * i + 4].reshape(GROUP, LANES)[:, 0:1]
        other = SJ[j, 0:1, 0:GROUP]
        student_gram = dot(i_rows(i, DT, DT + DS), j_rows(j, DT, DT + DS), ((1,), (1,)))
        d = jnp.clip(student_gram - total * own * other, -0.25, 0.25)
        D[i, j, :, :GROUP] = d.astype(jnp.bfloat16)

    arriving, forwards = {}, {}
    first = [
        push("S", X.at[OWN_J], X.at[J_INDEX[(0, 1)]]),
        push("S", SC.at[OWN_J], SC.at[J_INDEX[(0, 1)]]),
    ]

    def wait_slot(s):
        if s == 0:
            for copy in first:
                copy.wait()
        for copy in forwards.pop(s - 1, []):
            copy.wait()
        for copy in arriving.pop(("xy", s), []):
            copy.wait()
        for copy, m in arriving.pop(("z", s), []):
            copy.wait()
            if m is not None:
                forwards.setdefault(s, []).extend(
                    push_part("S", J_INDEX[(m[3], 0)], J_INDEX[(m[3], 1)], m[2])
                )

    for now in range(1, LAST + 1):
        if now > LAG - 1:
            wait_slot(now - LAG)
        for i, m in enumerate(MOVES):
            if SLOT[i] == now:
                arriving.setdefault(("xy", now), []).extend(
                    push_part(m[0], I_INDEX[m[1]], I_INDEX[m[3]], m[2])
                )
        for m in Z_MOVES:
            if m[4] == now:
                pair = push_part(m[0], J_INDEX[(m[1], 0)], J_INDEX[(m[3], 0)], m[2])
                arriving.setdefault(("z", now), []).extend((copy, m if copy is pair[-1] else None) for copy in pair)
        for task in TASKS[now]:
            run(task)
    for stage in range(LAST - LAG + 1, LAST):
        wait_slot(stage)
        for task in TASKS["after", stage]:
            run(task)
    for copy in forwards.pop(LAST - 1, []):
        copy.wait()
    for task in TASKS["after", LAST]:
        run(task)
    shared, waiting, z_waiting = {}, {}, {}

    def last(j):
        for task in TASKS["last", j]:
            run(task)
        grad_j(j)
        for d, core in reversed(J_ORDER[4 * j:4 * j + 4]):
            if core == 1:
                shared[d] = push("S", GJ.at[:, J_INDEX[(d, 1)] - 16], RS.at[d])

    def collect(i):
        if i not in waiting:
            return
        waiting.pop(i).wait()
        m = R_MOVES[i]
        GI[m[2], I_INDEX[m[3]]] += RI[i]

    def send_xy(i):
        m = R_MOVES[i]
        for f in R_FEEDS[i]:
            if f in waiting:
                collect(f)
        waiting[i] = push(m[0], GI.at[m[2], I_INDEX[m[1]]], RI.at[i])

    def z_collect(i):
        if i not in z_waiting:
            return
        z_waiting.pop(i).wait()
        m = RZ_MOVES[i]
        GJ[m[2], J_INDEX[(m[3], 0)] - 16] += RJ[i]

    def join(d):
        if d in shared:
            shared.pop(d).wait()
            GJ[:, J_INDEX[(d, 0)] - 16] += RS[d]

    def send_z(i):
        m = RZ_MOVES[i]
        join(m[1])
        for f in RZ_FEEDS[i]:
            if f in z_waiting:
                z_collect(f)
        z_waiting[i] = push(m[0], GJ.at[m[2], J_INDEX[(m[1], 0)] - 16], RJ.at[i])

    steps, clock, j_ready, i_ready = [(-0.1, 0, wait_slot, LAST)], 0.0, {}, [-1.0] * 4
    for n, j in enumerate((0, 3, 2, 1)):
        steps.append((clock, n, last, j))
        clock += 0.3 + 0.75 * len(TASKS["last", j])
        for d, core in J_ORDER[4 * j:4 * j + 4]:
            j_ready[d] = clock + S_HOP
    for i in TASKS["late"]:
        steps.append((clock, 4 + i, grad_i, i))
        clock += 0.3
        i_ready[i] = clock
    starts = timed(R_MOVES, R_FEEDS, [i_ready[I_INDEX[m[1]] // 4] for m in R_MOVES], [0.62] * len(R_MOVES))
    for i, at in starts.items():
        steps.append((at, 10 + i, send_xy, i))
        got = max(at + 0.62 + HOP, i_ready[I_INDEX[R_MOVES[i][3]] // 4])
        steps.append((got, 200 + i, collect, i))
    starts = timed(RZ_MOVES, RZ_FEEDS, [j_ready[m[1]] for m in RZ_MOVES], [0.62] * len(RZ_MOVES))
    for i, at in starts.items():
        steps.append((at, 100 + i, send_z, i))
        got = max(at + 0.62 + HOP, j_ready[RZ_MOVES[i][3]])
        steps.append((got, 300 + i, z_collect, i))
    for _, _, act, what in sorted(steps, key=lambda step: step[:2]):
        act(what)
    assert not arriving and not forwards
    join(0)
    factor = 4.0 / jnp.sqrt(jnp.float32(TEXTS))
    for q in range(4):
        out[:, q * QI:(q + 1) * QI] = factor * GI[q, I_INDEX[(0, 0)]]
    for h in range(4):
        out[:, WI + h * HJ:WI + (h + 1) * HJ] = factor * GJ[h, 0]


COPIES = 32 + len(MOVES) + 2 * len(Z_MOVES) + 8 + len(R_MOVES) + len(RZ_MOVES)


def per_device(student, teacher, scales):
    return pl.pallas_call(
        kernel,
        out_shape=jax.ShapeDtypeStruct((ROWS, DS), jnp.float32),
        in_specs=[
            pl.BlockSpec(memory_space=pl.ANY),
            pl.BlockSpec(memory_space=pl.ANY),
            pl.BlockSpec(memory_space=pltpu.VMEM),
        ],
        out_specs=pl.BlockSpec(memory_space=pltpu.VMEM),
        scratch_shapes=[
            pltpu.VMEM((BLOCKS, ROWS, WIDTH), jnp.bfloat16),
            pltpu.VMEM((BLOCKS, 8, LANES), jnp.float32),
            pltpu.VMEM((16, ROWS, LANES), jnp.float32),
            pltpu.VMEM((4, 8, 2 * LANES), jnp.float32),
            pltpu.VMEM((4, 4, GROUP, 256), jnp.float32),
            pltpu.VMEM((4, 4, GROUP, 256), jnp.bfloat16),
            pltpu.VMEM((4, 16, ROWS, QI), jnp.float32),
            pltpu.VMEM((4, 16, ROWS, HJ), jnp.float32),
            pltpu.VMEM((len(R_MOVES), ROWS, QI), jnp.float32),
            pltpu.VMEM((len(RZ_MOVES), ROWS, HJ), jnp.float32),
            pltpu.VMEM((8, 4, ROWS, HJ), jnp.float32),
            pltpu.SemaphoreType.DMA((4,)),
            pltpu.SemaphoreType.DMA((COPIES,)),
            pltpu.SemaphoreType.DMA((COPIES,)),
        ],
        compiler_params=pltpu.CompilerParams(
            collective_id=0, has_side_effects=True, vmem_limit_bytes=56 * 2**20
        ),
        cost_estimate=pl.CostEstimate(flops=10**10, bytes_accessed=10**6, transcendentals=0),
        name="huber_gram",
    )(student, teacher, scales.reshape(1, ROWS))


def solution(mesh):
    return jax.shard_map(
        per_device,
        mesh=mesh,
        in_specs=(P(("row", "col"), None), P(("row", "col"), None), P(("row", "col"))),
        out_specs=P(("row", "col"), None),
        check_vma=False,
    )
```

```python
import functools
import jax
import jax.numpy as jnp
from jax import lax
from jax.experimental import pallas as pl
from jax.experimental.pallas import tpu as pltpu
from jax.sharding import PartitionSpec as P

DS, DT, ROWS, LANES = 1024, 4096, 56, 128
TEXTS = 14336
WIDTH = DT + DS
PIECES = ((0, 1280), (1280, 2560), (2560, 3840), (3840, WIDTH))
T_PIECES = ((0, 1280), (1280, 2560), (2560, 3840), (3840, DT))
LINKS = ("X+", "X-", "Y+", "Y-", "Z+", "Z-", "S")
GROUP = 4 * ROWS
WI = 512
WJ = DS - WI
QI, HJ = WI // 4, WJ // 4
LAG = 2
BUDGET = 2.2
HOP = 2.2
S_HOP = 2.5


def moved(block, link):
    step = 1 if link[1] == "+" else -1
    if link[0] == "X":
        return ((block[0] - step) % 4, block[1])
    return (block[0], (block[1] - step) % 4)


def gather_xy():
    out = []

    def ring(axis, heads, p, q):
        for head in heads:
            for link, far, order in ((axis + "+", p, (p, q)), (axis + "-", q, (q, p))):
                near = moved(head, link)
                out.extend((link, head, piece, near) for piece in order)
                out.append((link, near, far, moved(near, link)))

    ring("X", [(0, 0)], 0, 1)
    ring("Y", [(d, 0) for d in (2, 1, 3, 0)], 0, 1)
    ring("Y", [(0, 0)], 2, 3)
    ring("X", [(0, d) for d in (2, 1, 3, 0)], 2, 3)
    return out


def slots_of(moves, feeds, links, lag):
    n = len(moves)
    users = [[j for j in range(n) if i in feeds[j]] for i in range(n)]

    @functools.cache
    def height(i):
        return 1 + max([height(j) for j in users[i]], default=0)

    slot, now = {}, 0
    while len(slot) < n:
        now += 1
        for link in links:
            ready = [
                i for i in range(n)
                if i not in slot and moves[i][0] == link
                and all(f in slot and slot[f] + lag <= now for f in feeds[i])
            ]
            if ready:
                best = min(ready, key=lambda i: (-height(i), -len(users[i]), not {moves[i][3][0], moves[i][3][1]} & {2}, i))
                slot[best] = now
    return slot


def plan_gather():
    moves = gather_xy()
    source = {(m[3], m[2]): i for i, m in enumerate(moves)}
    feeds = [[source[(m[1], m[2])]] if (m[1], m[2]) in source else [] for m in moves]
    slot = slots_of(moves, feeds, LINKS[:4], LAG)
    return moves, feeds, slot


MOVES, FEEDS, SLOT = plan_gather()
LAST = max(SLOT.values())
ARRIVE = {}
for _i, _m in enumerate(MOVES):
    ARRIVE.setdefault(_m[3], {})[_m[2]] = SLOT[_i]
ARRIVE[(0, 0)] = {p: 0 for p in range(4)}
I_ORDER = sorted(ARRIVE, key=lambda b: (max(ARRIVE[b].values()), sum(ARRIVE[b].values()), b))
I_INDEX = {b: i for i, b in enumerate(I_ORDER)}
J_ORDER = [(0, 0), (0, 1), (4, 0), (4, 1)]
for _d in (1, 2, 3):
    J_ORDER += [(_d, 0), (8 - _d, 0), (_d, 1), (8 - _d, 1)]
J_INDEX = {b: 16 + i for i, b in enumerate(J_ORDER)}
OWN, OWN_J = I_INDEX[(0, 0)], J_INDEX[(0, 0)]
BLOCKS = 32

Z_MOVES = []
for _s in range(14):
    _d, _p = _s // 4, _s % 4
    Z_MOVES.append(("Z+", (8 - _d) % 8, _p, 7 - _d, _s + 1))
    Z_MOVES.append(("Z-", _d, (_p + 2) % 4, _d + 1, _s + 1))
J_ARRIVE = {b: {p: 0 for p in range(4)} for b in J_ORDER}
for _m in Z_MOVES:
    J_ARRIVE[(_m[3], 0)][_m[2]] = _m[4]
    J_ARRIVE[(_m[3], 1)][_m[2]] = _m[4] + 1


FIRST = {(0, 0), (1, 0), (2, 0)}


def plan_compute():
    i_at = [[max(ARRIVE[b][p] for b in I_ORDER[4 * g:4 * g + 4]) for p in range(4)] for g in range(4)]
    j_at = [[max(J_ARRIVE[b][p] for b in J_ORDER[4 * g:4 * g + 4]) for p in range(4)] for g in range(4)]
    left = {(i, j): [0, 1, 2, 3] for i in range(4) for j in range(4)}
    started = set()
    done = {i: 0 for i in range(4)}
    out = {}

    def runs(pieces):
        ranges = []
        for p in pieces:
            if ranges and ranges[-1][1] == T_PIECES[p][0]:
                ranges[-1][1] = T_PIECES[p][1]
            else:
                ranges.append(list(T_PIECES[p]))
        return ranges

    def pick(seen, budget, least, j_seen=None, only=None):
        cost, tasks = 0.0, []
        while cost < budget:
            best = None
            for i, j in sorted(left if only is None else only & set(left)):
                ready = [p for p in left[(i, j)] if i_at[i][p] <= seen and j_at[j][p] <= (j_seen or seen)]
                final = len(ready) == len(left[(i, j)])
                ready = ready if final else [p for p in ready if p != 3]
                if final or len(ready) >= least:
                    key = (final, len(ready), -i)
                    if best is None or key > best[0]:
                        best = (key, i, j, ready, final)
            if best is None:
                break
            _, i, j, ready, final = best
            cost += 0.14 * len(ready) + (0.15 if final else 0.02)
            tasks.append(("final" if final else "acc", i, j, runs(ready), (i, j) in started))
            started.add((i, j))
            left[(i, j)] = [p for p in left[(i, j)] if p not in ready]
            if final:
                del left[(i, j)]
                done[i] += 1
                if done[i] == 4:
                    tasks.append(("grad", i))
                    cost += 0.3
        return tasks, cost

    for now in range(1, LAST + 1):
        out[now], _ = pick(now - LAG, BUDGET, 1 if now > LAST - 5 else 2)
    for stage in range(LAST - LAG + 1, LAST):
        out["after", stage], _ = pick(stage, 9.0, 1, None, FIRST if stage == LAST - 1 else None)
    out["after", LAST], _ = pick(LAST - 1, 9.0, 1, LAST, FIRST)
    for j in (0, 3, 2, 1):
        tasks = []
        for i in range(4):
            if (i, j) in left:
                tasks.append(("final", i, j, runs(left.pop((i, j))), (i, j) in started))
                done[i] += 1
        out["last", j] = tasks
    assert not left
    out["late"] = [i for i in range(4) if ("grad", i) not in sum((v for v in out.values() if isinstance(v, list)), [])]
    return out


TASKS = plan_compute()


def plan_reduce():
    moves = []

    def ring(axis, heads, p, q):
        def at(head, d):
            return ((head[0] + d) % 4, head[1]) if axis == "X" else (head[0], (head[1] + d) % 4)
        for head in heads:
            plus, minus = axis + "+", axis + "-"
            moves.append((plus, at(head, 2), p, at(head, 1)))
            moves.append((minus, at(head, 2), q, at(head, 3)))
            for piece in (q, p):
                moves.append((plus, at(head, 1), piece, head))
            for piece in (p, q):
                moves.append((minus, at(head, 3), piece, head))

    ring("Y", [(d, 0) for d in (2, 1, 3, 0)], 0, 1)
    ring("X", [(0, 0)], 0, 1)
    ring("X", [(0, d) for d in (2, 1, 3, 0)], 2, 3)
    ring("Y", [(0, 0)], 2, 3)
    feeds = [[j for j, f in enumerate(moves) if f[3] == m[1] and f[2] == m[2]] for m in moves]
    return moves, feeds


R_MOVES, R_FEEDS = plan_reduce()
RZ_MOVES = []
for _d in (4, 3, 2, 1):
    for _q in (0, 1):
        RZ_MOVES.append(("Z+", _d, _q, _d - 1))
        RZ_MOVES.append(("Z-", (8 - _d) % 8, 2 + _q, (9 - _d) % 8))
    for _q in (0, 1):
        if _d < 4:
            RZ_MOVES.append(("Z+", _d, 2 + _q, _d - 1))
            RZ_MOVES.append(("Z-", (8 - _d) % 8, _q, (9 - _d) % 8))
RZ_FEEDS = [[j for j, f in enumerate(RZ_MOVES) if f[3] == m[1] and f[2] == m[2]] for m in RZ_MOVES]


def timed(moves, feeds, ready, length):
    n = len(moves)
    users = [[j for j in range(n) if i in feeds[j]] for i in range(n)]

    @functools.cache
    def height(i):
        return 1 + max([height(j) for j in users[i]], default=0)

    start, free = {}, {}
    while len(start) < n:
        best = None
        for i in range(n):
            if i in start or any(f not in start for f in feeds[i]):
                continue
            at = max([ready[i], free.get(moves[i][0], -9.0)] + [start[f] + length[i] + HOP for f in feeds[i]])
            key = (at, -height(i), i)
            if best is None or key < best:
                best = key
        at, _, i = best
        start[i] = at
        free[moves[i][0]] = at + length[i]
    return start


def dot(a, b, dims):
    return lax.dot_general(a, b, ((dims[0], dims[1]), ((), ())), preferred_element_type=jnp.float32)


def kernel(student, teacher, scales, out, X, SC, SI, SJ, acc, D, GI, GJ, RI, RJ, RS, load_sem, send, recv):
    row, col = lax.axis_index("row"), lax.axis_index("col")
    z, c = row // 2, row % 2
    x, y = col // 4, col % 4
    peer = {
        "X+": (row, ((x + 1) % 4) * 4 + y), "X-": (row, ((x + 3) % 4) * 4 + y),
        "Y+": (row, x * 4 + (y + 1) % 4), "Y-": (row, x * 4 + (y + 3) % 4),
        "Z+": (((z + 1) % 8) * 2 + c, col), "Z-": (((z + 7) % 8) * 2 + c, col),
        "S": (z * 2 + 1 - c, col),
    }
    loads = [
        pltpu.make_async_copy(teacher, X.at[OWN, :, pl.ds(0, DT)], load_sem.at[0]),
        pltpu.make_async_copy(student, X.at[OWN, :, pl.ds(DT, DS)], load_sem.at[1]),
        pltpu.make_async_copy(teacher, X.at[OWN_J, :, pl.ds(0, DT)], load_sem.at[2]),
        pltpu.make_async_copy(student, X.at[OWN_J, :, pl.ds(DT, DS)], load_sem.at[3]),
    ]
    for load in loads:
        load.start()
    barrier = pltpu.get_barrier_semaphore()
    for link in LINKS:
        pl.semaphore_signal(barrier, inc=1, device_id=peer[link], device_id_type=pl.DeviceIdType.MESH)
    for own in (OWN, OWN_J):
        SC[own] = jnp.zeros((8, LANES), jnp.float32)
        SC[own, 0:1, 0:ROWS] = scales[...]
    for load in loads:
        load.wait()
    pl.semaphore_wait(barrier, len(LINKS))

    copies = []

    def push(link, src, dst):
        n = len(copies)
        copy = pltpu.make_async_remote_copy(
            src_ref=src, dst_ref=dst, send_sem=send.at[n], recv_sem=recv.at[n],
            device_id=peer[link], device_id_type=pl.DeviceIdType.MESH,
        )
        copy.start()
        copies.append(copy)
        return copy

    def part(index, piece):
        low_col, high_col = PIECES[piece]
        return X.at[index, :, pl.ds(low_col, high_col - low_col)]

    def push_part(link, src, dst, piece):
        out = [push(link, part(src, piece), part(dst, piece))]
        if piece == 3:
            out.append(push(link, SC.at[src], SC.at[dst]))
        return out

    def i_rows(g, a, b):
        return X[4 * g:4 * g + 4, :, a:b].reshape(GROUP, b - a)

    def j_rows(g, a, b):
        return X[16 + 4 * g:20 + 4 * g, :, a:b].reshape(GROUP, b - a)

    scaled = set()
    eye = lax.broadcasted_iota(jnp.int32, (ROWS, ROWS), 0) == lax.broadcasted_iota(jnp.int32, (ROWS, ROWS), 1)

    def grad_i(i):
        total = None
        for j in range(4):
            term = dot(D[i, j, :, :GROUP], j_rows(j, DT, DT + WI), ((1,), (0,)))
            total = term if total is None else total + term
        for q in range(4):
            GI[q, 4 * i:4 * i + 4] = total[:, q * QI:(q + 1) * QI].reshape(4, ROWS, QI)

    def grad_j(j):
        total = None
        for i in range(4):
            term = dot(D[i, j, :, :GROUP], i_rows(i, DT + WI, DT + DS), ((0,), (0,)))
            total = term if total is None else total + term
        for h in range(4):
            GJ[h, 4 * j:4 * j + 4] = total[:, h * HJ:(h + 1) * HJ].reshape(4, ROWS, HJ)

    def run(task):
        kind, i = task[:2]
        if kind == "grad":
            grad_i(i)
            return
        j, ranges, started = task[2:]
        total = acc[i, j, :, :GROUP] if started else None
        for a, b in ranges:
            term = dot(i_rows(i, a, b), j_rows(j, a, b), ((1,), (1,)))
            total = term if total is None else total + term
        if kind == "acc":
            acc[i, j, :, :GROUP] = total
            return
        if ("i", i) not in scaled:
            scaled.add(("i", i))
            for b in range(4 * i, 4 * i + 4):
                line = jnp.broadcast_to(SC[b, 0:1, 0:ROWS], (ROWS, ROWS))
                column = jnp.sum(jnp.where(eye, line, 0.0), axis=1, keepdims=True)
                SI[b] = jnp.broadcast_to(column, (ROWS, LANES))
        if ("j", j) not in scaled:
            scaled.add(("j", j))
            line = jnp.zeros((8, 2 * LANES), jnp.float32)
            for k in range(4):
                wide = jnp.concatenate([SC[16 + 4 * j + k], jnp.zeros((8, LANES), jnp.float32)], axis=1)
                line = line + (pltpu.roll(wide, ROWS * k, 1) if k else wide)
            SJ[j] = line
        own = SI[4 * i:4 * i + 4].reshape(GROUP, LANES)[:, 0:1]
        other = SJ[j, 0:1, 0:GROUP]
        student_gram = dot(i_rows(i, DT, DT + DS), j_rows(j, DT, DT + DS), ((1,), (1,)))
        d = jnp.clip(student_gram - total * own * other, -0.25, 0.25)
        D[i, j, :, :GROUP] = d.astype(jnp.bfloat16)

    arriving, forwards = {}, {}
    first = [
        push("S", X.at[OWN_J], X.at[J_INDEX[(0, 1)]]),
        push("S", SC.at[OWN_J], SC.at[J_INDEX[(0, 1)]]),
    ]

    def wait_slot(s):
        if s == 0:
            for copy in first:
                copy.wait()
        for copy in forwards.pop(s - 1, []):
            copy.wait()
        for copy in arriving.pop(("xy", s), []):
            copy.wait()
        for copy, m in arriving.pop(("z", s), []):
            copy.wait()
            if m is not None:
                forwards.setdefault(s, []).extend(
                    push_part("S", J_INDEX[(m[3], 0)], J_INDEX[(m[3], 1)], m[2])
                )

    for now in range(1, LAST + 1):
        if now > LAG - 1:
            wait_slot(now - LAG)
        for i, m in enumerate(MOVES):
            if SLOT[i] == now:
                arriving.setdefault(("xy", now), []).extend(
                    push_part(m[0], I_INDEX[m[1]], I_INDEX[m[3]], m[2])
                )
        for m in Z_MOVES:
            if m[4] == now:
                pair = push_part(m[0], J_INDEX[(m[1], 0)], J_INDEX[(m[3], 0)], m[2])
                arriving.setdefault(("z", now), []).extend((copy, m if copy is pair[-1] else None) for copy in pair)
        for task in TASKS[now]:
            run(task)
    for stage in range(LAST - LAG + 1, LAST):
        wait_slot(stage)
        for task in TASKS["after", stage]:
            run(task)
    for copy in forwards.pop(LAST - 1, []):
        copy.wait()
    for task in TASKS["after", LAST]:
        run(task)
    shared, waiting, z_waiting = {}, {}, {}

    def last(j):
        for task in TASKS["last", j]:
            run(task)
        grad_j(j)
        for d, core in reversed(J_ORDER[4 * j:4 * j + 4] if j else J_ORDER[2:4]):
            if core == 1:
                shared[d] = push("S", GJ.at[:, J_INDEX[(d, 1)] - 16], RS.at[d])

    def share(d):
        shared[d] = push("S", GJ.at[:, J_INDEX[(d, 1)] - 16], RS.at[d])

    def collect(i):
        if i not in waiting:
            return
        waiting.pop(i).wait()
        m = R_MOVES[i]
        GI[m[2], I_INDEX[m[3]]] += RI[i]

    def send_xy(i):
        m = R_MOVES[i]
        for f in R_FEEDS[i]:
            if f in waiting:
                collect(f)
        waiting[i] = push(m[0], GI.at[m[2], I_INDEX[m[1]]], RI.at[i])

    def z_collect(i):
        if i not in z_waiting:
            return
        z_waiting.pop(i).wait()
        m = RZ_MOVES[i]
        GJ[m[2], J_INDEX[(m[3], 0)] - 16] += RJ[i]

    def join(d):
        if d in shared:
            shared.pop(d).wait()
            GJ[:, J_INDEX[(d, 0)] - 16] += RS[d]

    def send_z(i):
        m = RZ_MOVES[i]
        join(m[1])
        for f in RZ_FEEDS[i]:
            if f in z_waiting:
                z_collect(f)
        z_waiting[i] = push(m[0], GJ.at[m[2], J_INDEX[(m[1], 0)] - 16], RJ.at[i])

    steps, clock, j_ready, i_ready = [(-0.1, 0, wait_slot, LAST)], 0.0, {}, [-1.0] * 4
    for n, j in enumerate((0, 3, 2, 1)):
        steps.append((clock, n, last, j))
        clock += 0.3 + 0.75 * len(TASKS["last", j])
        for d, core in J_ORDER[4 * j:4 * j + 4]:
            j_ready[d] = clock + S_HOP
    steps.append((clock, 9, share, 0))
    for i in TASKS["late"]:
        steps.append((clock, 4 + i, grad_i, i))
        clock += 0.3
        i_ready[i] = clock
    starts = timed(R_MOVES, R_FEEDS, [i_ready[I_INDEX[m[1]] // 4] for m in R_MOVES], [0.62] * len(R_MOVES))
    for i, at in starts.items():
        steps.append((at, 10 + i, send_xy, i))
        got = max(at + 0.62 + HOP, i_ready[I_INDEX[R_MOVES[i][3]] // 4])
        steps.append((got, 200 + i, collect, i))
    starts = timed(RZ_MOVES, RZ_FEEDS, [j_ready[m[1]] for m in RZ_MOVES], [0.62] * len(RZ_MOVES))
    for i, at in starts.items():
        steps.append((at, 100 + i, send_z, i))
        got = max(at + 0.62 + HOP, j_ready[RZ_MOVES[i][3]])
        steps.append((got, 300 + i, z_collect, i))
    for _, _, act, what in sorted(steps, key=lambda step: step[:2]):
        act(what)
    assert not arriving and not forwards
    join(0)
    factor = 4.0 / jnp.sqrt(jnp.float32(TEXTS))
    for q in range(4):
        out[:, q * QI:(q + 1) * QI] = factor * GI[q, I_INDEX[(0, 0)]]
    for h in range(4):
        out[:, WI + h * HJ:WI + (h + 1) * HJ] = factor * GJ[h, 0]


COPIES = 32 + len(MOVES) + 2 * len(Z_MOVES) + 8 + len(R_MOVES) + len(RZ_MOVES)


def per_device(student, teacher, scales):
    return pl.pallas_call(
        kernel,
        out_shape=jax.ShapeDtypeStruct((ROWS, DS), jnp.float32),
        in_specs=[
            pl.BlockSpec(memory_space=pl.ANY),
            pl.BlockSpec(memory_space=pl.ANY),
            pl.BlockSpec(memory_space=pltpu.VMEM),
        ],
        out_specs=pl.BlockSpec(memory_space=pltpu.VMEM),
        scratch_shapes=[
            pltpu.VMEM((BLOCKS, ROWS, WIDTH), jnp.bfloat16),
            pltpu.VMEM((BLOCKS, 8, LANES), jnp.float32),
            pltpu.VMEM((16, ROWS, LANES), jnp.float32),
            pltpu.VMEM((4, 8, 2 * LANES), jnp.float32),
            pltpu.VMEM((4, 4, GROUP, 256), jnp.float32),
            pltpu.VMEM((4, 4, GROUP, 256), jnp.bfloat16),
            pltpu.VMEM((4, 16, ROWS, QI), jnp.float32),
            pltpu.VMEM((4, 16, ROWS, HJ), jnp.float32),
            pltpu.VMEM((len(R_MOVES), ROWS, QI), jnp.float32),
            pltpu.VMEM((len(RZ_MOVES), ROWS, HJ), jnp.float32),
            pltpu.VMEM((8, 4, ROWS, HJ), jnp.float32),
            pltpu.SemaphoreType.DMA((4,)),
            pltpu.SemaphoreType.DMA((COPIES,)),
            pltpu.SemaphoreType.DMA((COPIES,)),
        ],
        compiler_params=pltpu.CompilerParams(
            collective_id=0, has_side_effects=True, vmem_limit_bytes=56 * 2**20
        ),
        cost_estimate=pl.CostEstimate(flops=10**10, bytes_accessed=10**6, transcendentals=0),
        name="huber_gram",
    )(student, teacher, scales.reshape(1, ROWS))


def solution(mesh):
    return jax.shard_map(
        per_device,
        mesh=mesh,
        in_specs=(P(("row", "col"), None), P(("row", "col"), None), P(("row", "col"))),
        out_specs=P(("row", "col"), None),
        check_vma=False,
    )
```

```python
import functools
import jax
import jax.numpy as jnp
from jax import lax
from jax.experimental import pallas as pl
from jax.experimental.pallas import tpu as pltpu
from jax.sharding import PartitionSpec as P

DS, DT, ROWS, LANES = 1024, 4096, 56, 128
TEXTS = 14336
WIDTH = DT + DS
PIECES = ((0, 1280), (1280, 2560), (2560, 3840), (3840, WIDTH))
T_PIECES = ((0, 1280), (1280, 2560), (2560, 3840), (3840, DT))
LINKS = ("X+", "X-", "Y+", "Y-", "Z+", "Z-", "S")
GROUP = 4 * ROWS
WI = 512
WJ = DS - WI
QI, HJ = WI // 4, WJ // 4
LAG = 3
BUDGET = 2.2
HOP = 1.5
S_HOP = 1.5


def moved(block, link):
    step = 1 if link[1] == "+" else -1
    if link[0] == "X":
        return ((block[0] - step) % 4, block[1])
    return (block[0], (block[1] - step) % 4)


def gather_xy():
    out = []

    def ring(axis, heads, p, q):
        for head in heads:
            for link, far, order in ((axis + "+", p, (p, q)), (axis + "-", q, (q, p))):
                near = moved(head, link)
                out.extend((link, head, piece, near) for piece in order)
                out.append((link, near, far, moved(near, link)))

    ring("X", [(0, 0)], 0, 1)
    ring("Y", [(d, 0) for d in (2, 1, 3, 0)], 0, 1)
    ring("Y", [(0, 0)], 2, 3)
    ring("X", [(0, d) for d in (2, 1, 3, 0)], 2, 3)
    return out


def slots_of(moves, feeds, links, lag):
    n = len(moves)
    users = [[j for j in range(n) if i in feeds[j]] for i in range(n)]

    @functools.cache
    def height(i):
        return 1 + max([height(j) for j in users[i]], default=0)

    slot, now = {}, 0
    while len(slot) < n:
        now += 1
        for link in links:
            ready = [
                i for i in range(n)
                if i not in slot and moves[i][0] == link
                and all(f in slot and slot[f] + lag <= now for f in feeds[i])
            ]
            if ready:
                best = min(ready, key=lambda i: (-height(i), -len(users[i]), not {moves[i][3][0], moves[i][3][1]} & {2}, i))
                slot[best] = now
    return slot


def plan_gather():
    moves = gather_xy()
    source = {(m[3], m[2]): i for i, m in enumerate(moves)}
    feeds = [[source[(m[1], m[2])]] if (m[1], m[2]) in source else [] for m in moves]
    slot = slots_of(moves, feeds, LINKS[:4], LAG)
    return moves, feeds, slot


MOVES, FEEDS, SLOT = plan_gather()
LAST = max(SLOT.values())
ARRIVE = {}
for _i, _m in enumerate(MOVES):
    ARRIVE.setdefault(_m[3], {})[_m[2]] = SLOT[_i]
ARRIVE[(0, 0)] = {p: 0 for p in range(4)}
I_ORDER = sorted(ARRIVE, key=lambda b: (max(ARRIVE[b].values()), sum(ARRIVE[b].values()), b))
I_INDEX = {b: i for i, b in enumerate(I_ORDER)}
J_ORDER = [(0, 0), (0, 1), (4, 0), (4, 1)]
for _d in (1, 2, 3):
    J_ORDER += [(_d, 0), (8 - _d, 0), (_d, 1), (8 - _d, 1)]
J_INDEX = {b: 16 + i for i, b in enumerate(J_ORDER)}
OWN, OWN_J = I_INDEX[(0, 0)], J_INDEX[(0, 0)]
BLOCKS = 32

Z_MOVES = []
for _s in range(14):
    _d, _p = _s // 4, _s % 4
    Z_MOVES.append(("Z+", (8 - _d) % 8, _p, 7 - _d, _s + 1))
    Z_MOVES.append(("Z-", _d, (_p + 2) % 4, _d + 1, _s + 1))
J_ARRIVE = {b: {p: 0 for p in range(4)} for b in J_ORDER}
for _m in Z_MOVES:
    J_ARRIVE[(_m[3], 0)][_m[2]] = _m[4]
    J_ARRIVE[(_m[3], 1)][_m[2]] = _m[4] + 1


FIRST = {(0, 0), (1, 0), (2, 0)}


def plan_compute():
    i_at = [[max(ARRIVE[b][p] for b in I_ORDER[4 * g:4 * g + 4]) for p in range(4)] for g in range(4)]
    j_at = [[max(J_ARRIVE[b][p] for b in J_ORDER[4 * g:4 * g + 4]) for p in range(4)] for g in range(4)]
    left = {(i, j): [0, 1, 2, 3] for i in range(4) for j in range(4)}
    started = set()
    done = {i: 0 for i in range(4)}
    out = {}

    def runs(pieces):
        ranges = []
        for p in pieces:
            if ranges and ranges[-1][1] == T_PIECES[p][0]:
                ranges[-1][1] = T_PIECES[p][1]
            else:
                ranges.append(list(T_PIECES[p]))
        return ranges

    def pick(seen, budget, least, j_seen=None, only=None):
        cost, tasks = 0.0, []
        while cost < budget:
            best = None
            for i, j in sorted(left if only is None else only & set(left)):
                ready = [p for p in left[(i, j)] if i_at[i][p] <= seen and j_at[j][p] <= (j_seen or seen)]
                final = len(ready) == len(left[(i, j)])
                ready = ready if final else [p for p in ready if p != 3]
                if final or len(ready) >= least:
                    key = (final, len(ready), -i)
                    if best is None or key > best[0]:
                        best = (key, i, j, ready, final)
            if best is None:
                break
            _, i, j, ready, final = best
            cost += 0.14 * len(ready) + (0.15 if final else 0.02)
            tasks.append(("final" if final else "acc", i, j, runs(ready), (i, j) in started))
            started.add((i, j))
            left[(i, j)] = [p for p in left[(i, j)] if p not in ready]
            if final:
                del left[(i, j)]
                done[i] += 1
                if done[i] == 4:
                    tasks.append(("grad", i))
                    cost += 0.3
        return tasks, cost

    for now in range(1, LAST + 1):
        out[now], _ = pick(now - LAG, BUDGET, 1 if now > LAST - 5 else 2)
    for stage in range(LAST - LAG + 1, LAST):
        out["after", stage], _ = pick(stage, 9.0, 1, None, FIRST if stage == LAST - 1 else None)
    out["after", LAST], _ = pick(LAST - 1, 9.0, 1, LAST, FIRST)
    for j in (0, 3, 2, 1):
        tasks = []
        for i in range(4):
            if (i, j) in left:
                tasks.append(("final", i, j, runs(left.pop((i, j))), (i, j) in started))
                done[i] += 1
        out["last", j] = tasks
    assert not left
    out["late"] = [i for i in range(4) if ("grad", i) not in sum((v for v in out.values() if isinstance(v, list)), [])]
    return out


TASKS = plan_compute()


def plan_reduce():
    moves = []

    def ring(axis, heads, p, q):
        def at(head, d):
            return ((head[0] + d) % 4, head[1]) if axis == "X" else (head[0], (head[1] + d) % 4)
        for head in heads:
            plus, minus = axis + "+", axis + "-"
            moves.append((plus, at(head, 2), p, at(head, 1)))
            moves.append((minus, at(head, 2), q, at(head, 3)))
            for piece in (q, p):
                moves.append((plus, at(head, 1), piece, head))
            for piece in (p, q):
                moves.append((minus, at(head, 3), piece, head))

    ring("Y", [(d, 0) for d in (2, 1, 3, 0)], 0, 1)
    ring("X", [(0, 0)], 0, 1)
    ring("X", [(0, d) for d in (2, 1, 3, 0)], 2, 3)
    ring("Y", [(0, 0)], 2, 3)
    feeds = [[j for j, f in enumerate(moves) if f[3] == m[1] and f[2] == m[2]] for m in moves]
    return moves, feeds


R_MOVES, R_FEEDS = plan_reduce()
RZ_MOVES = []
for _d in (4, 3, 2, 1):
    for _q in (0, 1):
        RZ_MOVES.append(("Z+", _d, _q, _d - 1))
        RZ_MOVES.append(("Z-", (8 - _d) % 8, 2 + _q, (9 - _d) % 8))
    for _q in (0, 1):
        if _d < 4:
            RZ_MOVES.append(("Z+", _d, 2 + _q, _d - 1))
            RZ_MOVES.append(("Z-", (8 - _d) % 8, _q, (9 - _d) % 8))
RZ_FEEDS = [[j for j, f in enumerate(RZ_MOVES) if f[3] == m[1] and f[2] == m[2]] for m in RZ_MOVES]


def timed(moves, feeds, ready, length):
    n = len(moves)
    users = [[j for j in range(n) if i in feeds[j]] for i in range(n)]

    @functools.cache
    def height(i):
        return 1 + max([height(j) for j in users[i]], default=0)

    start, free = {}, {}
    while len(start) < n:
        best = None
        for i in range(n):
            if i in start or any(f not in start for f in feeds[i]):
                continue
            at = max([ready[i], free.get(moves[i][0], -9.0)] + [start[f] + length[i] + HOP for f in feeds[i]])
            key = (at, -height(i), i)
            if best is None or key < best:
                best = key
        at, _, i = best
        start[i] = at
        free[moves[i][0]] = at + length[i]
    return start


def dot(a, b, dims):
    return lax.dot_general(a, b, ((dims[0], dims[1]), ((), ())), preferred_element_type=jnp.float32)


def kernel(student, teacher, scales, out, X, SC, SI, SJ, acc, D, GI, GJ, RI, RJ, RS, load_sem, send, recv):
    row, col = lax.axis_index("row"), lax.axis_index("col")
    z, c = row // 2, row % 2
    x, y = col // 4, col % 4
    peer = {
        "X+": (row, ((x + 1) % 4) * 4 + y), "X-": (row, ((x + 3) % 4) * 4 + y),
        "Y+": (row, x * 4 + (y + 1) % 4), "Y-": (row, x * 4 + (y + 3) % 4),
        "Z+": (((z + 1) % 8) * 2 + c, col), "Z-": (((z + 7) % 8) * 2 + c, col),
        "S": (z * 2 + 1 - c, col),
    }
    loads = [
        pltpu.make_async_copy(teacher, X.at[OWN, :, pl.ds(0, DT)], load_sem.at[0]),
        pltpu.make_async_copy(student, X.at[OWN, :, pl.ds(DT, DS)], load_sem.at[1]),
        pltpu.make_async_copy(teacher, X.at[OWN_J, :, pl.ds(0, DT)], load_sem.at[2]),
        pltpu.make_async_copy(student, X.at[OWN_J, :, pl.ds(DT, DS)], load_sem.at[3]),
    ]
    for load in loads:
        load.start()
    barrier = pltpu.get_barrier_semaphore()
    for link in LINKS:
        pl.semaphore_signal(barrier, inc=1, device_id=peer[link], device_id_type=pl.DeviceIdType.MESH)
    for own in (OWN, OWN_J):
        SC[own] = jnp.zeros((8, LANES), jnp.float32)
        SC[own, 0:1, 0:ROWS] = scales[...]
    for load in loads:
        load.wait()
    pl.semaphore_wait(barrier, len(LINKS))

    copies = []

    def push(link, src, dst):
        n = len(copies)
        copy = pltpu.make_async_remote_copy(
            src_ref=src, dst_ref=dst, send_sem=send.at[n], recv_sem=recv.at[n],
            device_id=peer[link], device_id_type=pl.DeviceIdType.MESH,
        )
        copy.start()
        copies.append(copy)
        return copy

    def part(index, piece):
        low_col, high_col = PIECES[piece]
        return X.at[index, :, pl.ds(low_col, high_col - low_col)]

    def push_part(link, src, dst, piece):
        out = [push(link, part(src, piece), part(dst, piece))]
        if piece == 3:
            out.append(push(link, SC.at[src], SC.at[dst]))
        return out

    def i_rows(g, a, b):
        return X[4 * g:4 * g + 4, :, a:b].reshape(GROUP, b - a)

    def j_rows(g, a, b):
        return X[16 + 4 * g:20 + 4 * g, :, a:b].reshape(GROUP, b - a)

    scaled = set()
    eye = lax.broadcasted_iota(jnp.int32, (ROWS, ROWS), 0) == lax.broadcasted_iota(jnp.int32, (ROWS, ROWS), 1)

    def grad_i(i):
        total = None
        for j in range(4):
            term = dot(D[i, j, :, :GROUP], j_rows(j, DT, DT + WI), ((1,), (0,)))
            total = term if total is None else total + term
        for q in range(4):
            GI[q, 4 * i:4 * i + 4] = total[:, q * QI:(q + 1) * QI].reshape(4, ROWS, QI)

    def grad_j(j):
        total = None
        for i in range(4):
            term = dot(D[i, j, :, :GROUP], i_rows(i, DT + WI, DT + DS), ((0,), (0,)))
            total = term if total is None else total + term
        for h in range(4):
            GJ[h, 4 * j:4 * j + 4] = total[:, h * HJ:(h + 1) * HJ].reshape(4, ROWS, HJ)

    def run(task):
        kind, i = task[:2]
        if kind == "grad":
            grad_i(i)
            return
        j, ranges, started = task[2:]
        total = acc[i, j, :, :GROUP] if started else None
        for a, b in ranges:
            term = dot(i_rows(i, a, b), j_rows(j, a, b), ((1,), (1,)))
            total = term if total is None else total + term
        if kind == "acc":
            acc[i, j, :, :GROUP] = total
            return
        if ("i", i) not in scaled:
            scaled.add(("i", i))
            for b in range(4 * i, 4 * i + 4):
                line = jnp.broadcast_to(SC[b, 0:1, 0:ROWS], (ROWS, ROWS))
                column = jnp.sum(jnp.where(eye, line, 0.0), axis=1, keepdims=True)
                SI[b] = jnp.broadcast_to(column, (ROWS, LANES))
        if ("j", j) not in scaled:
            scaled.add(("j", j))
            line = jnp.zeros((8, 2 * LANES), jnp.float32)
            for k in range(4):
                wide = jnp.concatenate([SC[16 + 4 * j + k], jnp.zeros((8, LANES), jnp.float32)], axis=1)
                line = line + (pltpu.roll(wide, ROWS * k, 1) if k else wide)
            SJ[j] = line
        own = SI[4 * i:4 * i + 4].reshape(GROUP, LANES)[:, 0:1]
        other = SJ[j, 0:1, 0:GROUP]
        student_gram = dot(i_rows(i, DT, DT + DS), j_rows(j, DT, DT + DS), ((1,), (1,)))
        d = jnp.clip(student_gram - total * own * other, -0.25, 0.25)
        D[i, j, :, :GROUP] = d.astype(jnp.bfloat16)

    arriving, forwards = {}, {}
    first = [
        push("S", X.at[OWN_J], X.at[J_INDEX[(0, 1)]]),
        push("S", SC.at[OWN_J], SC.at[J_INDEX[(0, 1)]]),
    ]

    def wait_slot(s):
        if s == 0:
            for copy in first:
                copy.wait()
        for copy in forwards.pop(s - 1, []):
            copy.wait()
        for copy in arriving.pop(("xy", s), []):
            copy.wait()
        for copy, m in arriving.pop(("z", s), []):
            copy.wait()
            if m is not None:
                forwards.setdefault(s, []).extend(
                    push_part("S", J_INDEX[(m[3], 0)], J_INDEX[(m[3], 1)], m[2])
                )

    for now in range(1, LAST + 1):
        if now > LAG - 1:
            wait_slot(now - LAG)
        for i, m in enumerate(MOVES):
            if SLOT[i] == now:
                arriving.setdefault(("xy", now), []).extend(
                    push_part(m[0], I_INDEX[m[1]], I_INDEX[m[3]], m[2])
                )
        for m in Z_MOVES:
            if m[4] == now:
                pair = push_part(m[0], J_INDEX[(m[1], 0)], J_INDEX[(m[3], 0)], m[2])
                arriving.setdefault(("z", now), []).extend((copy, m if copy is pair[-1] else None) for copy in pair)
        for task in TASKS[now]:
            run(task)
    for stage in range(LAST - LAG + 1, LAST):
        wait_slot(stage)
        for task in TASKS["after", stage]:
            run(task)
    for copy in forwards.pop(LAST - 1, []):
        copy.wait()
    for task in TASKS["after", LAST]:
        run(task)
    shared, waiting, z_waiting = {}, {}, {}

    def last(j):
        for task in TASKS["last", j]:
            run(task)
        grad_j(j)
        for d, core in reversed(J_ORDER[4 * j:4 * j + 4]):
            if core == 1:
                shared[d] = push("S", GJ.at[:, J_INDEX[(d, 1)] - 16], RS.at[d])

    def collect(i):
        if i not in waiting:
            return
        waiting.pop(i).wait()
        m = R_MOVES[i]
        GI[m[2], I_INDEX[m[3]]] += RI[i]

    def send_xy(i):
        m = R_MOVES[i]
        for f in R_FEEDS[i]:
            if f in waiting:
                collect(f)
        waiting[i] = push(m[0], GI.at[m[2], I_INDEX[m[1]]], RI.at[i])

    def z_collect(i):
        if i not in z_waiting:
            return
        z_waiting.pop(i).wait()
        m = RZ_MOVES[i]
        GJ[m[2], J_INDEX[(m[3], 0)] - 16] += RJ[i]

    def join(d):
        if d in shared:
            shared.pop(d).wait()
            GJ[:, J_INDEX[(d, 0)] - 16] += RS[d]

    def send_z(i):
        m = RZ_MOVES[i]
        join(m[1])
        for f in RZ_FEEDS[i]:
            if f in z_waiting:
                z_collect(f)
        z_waiting[i] = push(m[0], GJ.at[m[2], J_INDEX[(m[1], 0)] - 16], RJ.at[i])

    steps, clock, j_ready, i_ready = [(-0.1, 0, wait_slot, LAST)], 0.0, {}, [-1.0] * 4
    for n, j in enumerate((0, 3, 2, 1)):
        steps.append((clock, n, last, j))
        clock += 0.3 + 0.75 * len(TASKS["last", j])
        for d, core in J_ORDER[4 * j:4 * j + 4]:
            j_ready[d] = clock + S_HOP
    for i in TASKS["late"]:
        steps.append((clock, 4 + i, grad_i, i))
        clock += 0.3
        i_ready[i] = clock
    starts = timed(R_MOVES, R_FEEDS, [i_ready[I_INDEX[m[1]] // 4] for m in R_MOVES], [0.62] * len(R_MOVES))
    for i, at in starts.items():
        steps.append((at, 10 + i, send_xy, i))
        got = max(at + 0.62 + HOP, i_ready[I_INDEX[R_MOVES[i][3]] // 4])
        steps.append((got, 200 + i, collect, i))
    starts = timed(RZ_MOVES, RZ_FEEDS, [j_ready[m[1]] for m in RZ_MOVES], [0.62] * len(RZ_MOVES))
    for i, at in starts.items():
        steps.append((at, 100 + i, send_z, i))
        got = max(at + 0.62 + HOP, j_ready[RZ_MOVES[i][3]])
        steps.append((got, 300 + i, z_collect, i))
    for _, _, act, what in sorted(steps, key=lambda step: step[:2]):
        act(what)
    assert not arriving and not forwards
    join(0)
    factor = 4.0 / jnp.sqrt(jnp.float32(TEXTS))
    for q in range(4):
        out[:, q * QI:(q + 1) * QI] = factor * GI[q, I_INDEX[(0, 0)]]
    for h in range(4):
        out[:, WI + h * HJ:WI + (h + 1) * HJ] = factor * GJ[h, 0]


COPIES = 32 + len(MOVES) + 2 * len(Z_MOVES) + 8 + len(R_MOVES) + len(RZ_MOVES)


def per_device(student, teacher, scales):
    return pl.pallas_call(
        kernel,
        out_shape=jax.ShapeDtypeStruct((ROWS, DS), jnp.float32),
        in_specs=[
            pl.BlockSpec(memory_space=pl.ANY),
            pl.BlockSpec(memory_space=pl.ANY),
            pl.BlockSpec(memory_space=pltpu.VMEM),
        ],
        out_specs=pl.BlockSpec(memory_space=pltpu.VMEM),
        scratch_shapes=[
            pltpu.VMEM((BLOCKS, ROWS, WIDTH), jnp.bfloat16),
            pltpu.VMEM((BLOCKS, 8, LANES), jnp.float32),
            pltpu.VMEM((16, ROWS, LANES), jnp.float32),
            pltpu.VMEM((4, 8, 2 * LANES), jnp.float32),
            pltpu.VMEM((4, 4, GROUP, 256), jnp.float32),
            pltpu.VMEM((4, 4, GROUP, 256), jnp.bfloat16),
            pltpu.VMEM((4, 16, ROWS, QI), jnp.float32),
            pltpu.VMEM((4, 16, ROWS, HJ), jnp.float32),
            pltpu.VMEM((len(R_MOVES), ROWS, QI), jnp.float32),
            pltpu.VMEM((len(RZ_MOVES), ROWS, HJ), jnp.float32),
            pltpu.VMEM((8, 4, ROWS, HJ), jnp.float32),
            pltpu.SemaphoreType.DMA((4,)),
            pltpu.SemaphoreType.DMA((COPIES,)),
            pltpu.SemaphoreType.DMA((COPIES,)),
        ],
        compiler_params=pltpu.CompilerParams(
            collective_id=0, has_side_effects=True, vmem_limit_bytes=56 * 2**20
        ),
        cost_estimate=pl.CostEstimate(flops=10**10, bytes_accessed=10**6, transcendentals=0),
        name="huber_gram",
    )(student, teacher, scales.reshape(1, ROWS))


def solution(mesh):
    return jax.shard_map(
        per_device,
        mesh=mesh,
        in_specs=(P(("row", "col"), None), P(("row", "col"), None), P(("row", "col"))),
        out_specs=P(("row", "col"), None),
        check_vma=False,
    )
```
